256 devices in a mesh: dp: 4 (over z_hi, core), section: 16 (over y, z_lo), tensor: 4 (over x).
Axes of the slice: x: 4, y: 4, z: 8 (z_hi: 2, z_lo: 4; z = z_hi * 4 + z_lo), core: 2. Of those that a mesh axis runs over, the one named last changes fastest.
Arguments:
- x_in: bfloat16 [16, 2048, 4096], P('section', ('dp', 'tensor')), may hold values from -6 to 6
- gain: bfloat16 [16, 4096], P('section'), may hold values from 0.5 to 1.5
- weight: bfloat16 [16, 4096, 4096], P('section', 'dp', 'tensor'), may hold values from -0.09375 to 0.09375
- moment_one: bfloat16 [16, 4096, 4096], P('section', 'dp', 'tensor'), may hold values from -0.039794922 to 0.039794922
- moment_two: bfloat16 [16, 4096, 4096], P('section', 'dp', 'tensor'), may hold values from 1.9907951e-05 to 0.00029945374
- cotangent: bfloat16 [16, 2048, 4096], P('section', ('dp', 'tensor')), may hold values from -6 to 6
- preempted: int32 [4, 16], replicated, may hold values from 0 to 1, as said below
Outputs:
- y_out: bfloat16 [16, 2048, 4096], P('section', ('dp', 'tensor'))
- dx_out: bfloat16 [16, 2048, 4096], P('section', ('dp', 'tensor'))
- update: bfloat16 [16, 4096, 4096], P('section', 'dp', 'tensor')
The draws below stay inside these ranges and needn't reach their ends.
Inputs may be any that keep to these rules, and one draw needn't show every extreme that they name: No two sections of one data group that are neighbours in the loop of 16 sections are both preempted, and data group 0 has at least one preempted section.
All inputs are finite; a program needn't handle non-finite values.
Results may differ from the reference program's by a relative error of at most 0.03.
Values may be sent and summed in bfloat16 or wider, within the bound.
A program may use at most 128 MiB of HBM per device.

```python
import math
import jax
import jax.numpy as jnp
from jax import lax

D = 4096
TOK_DEV = 128
SECTIONS = 16
ROWS = 2048
N_DP = 4
N_TENSOR = 4


def draw_preempted(key, part):
    key = jax.random.fold_in(key, 7)
    key_bits, key_pick = jax.random.split(key)
    picks = jax.random.randint(key_bits, (N_DP, SECTIONS), 0, 2).astype(jnp.int32)
    before = jnp.roll(picks, 1, axis=1)
    picks = (picks * (1 - before)).astype(jnp.int32)
    chosen = jax.random.randint(key_pick, (), 0, SECTIONS).astype(jnp.int32)
    section_ids = jnp.arange(SECTIONS, dtype=jnp.int32)
    offset = (section_ids - chosen) % SECTIONS
    near = jnp.logical_or(jnp.logical_or(offset == 0, offset == 1), offset == SECTIONS - 1).astype(jnp.int32)
    marker = (offset == 0).astype(jnp.int32)
    row_zero = picks[0] * (1 - near) + marker
    return picks.at[0].set(row_zero).astype(jnp.int32)


def block_levels(stream_key, shape, shards, smallest, top_value):
    factor_of, own = 1.0, jax.random.fold_in(stream_key, 6)
    for position, blocks in shards:
        steps = jnp.exp(jax.random.uniform(jax.random.fold_in(own, position), (blocks,), jnp.float32, smallest / len(shards), top_value / len(shards)))
        factor_of = factor_of * jnp.repeat(steps, shape[position] // blocks).reshape([-1 if axis == position else 1 for axis in range(len(shape))])
    return factor_of


def normal_values(stream_key, shape, deviation, limit, cuts=(), kind=jnp.bfloat16):
    entries = deviation * jax.random.normal(stream_key, shape, jnp.float32)
    if cuts:
        entries = entries * block_levels(stream_key, shape, cuts, -0.22, 0.18)
    return jnp.clip(entries, -limit, limit).astype(kind)


def setup_inputs(seed: int = 0) -> dict:
    splits = jax.random.split(jax.random.key(seed), 8)
    x_in = normal_values(splits[0], (SECTIONS, ROWS, D), 1.0, 6.0, ((0, 16), (1, 16)))
    gain = jnp.clip(1.0 + 0.1 * jax.random.normal(splits[1], (SECTIONS, D), jnp.float32), 0.5, 1.5).astype(jnp.bfloat16)
    weight = normal_values(splits[2], (SECTIONS, D, D), D ** -0.5, 0.09375, ((0, 16), (1, 4), (2, 4)))
    moment_one = normal_values(splits[3], (SECTIONS, D, D), 0.01, 0.039794922, ((0, 16), (1, 4), (2, 4)))
    moment_two = jnp.clip(jnp.exp(math.log(0.00029945374) - 2.7108407 * jax.random.uniform(splits[4], (SECTIONS, D, D), jnp.float32) ** block_levels(splits[4], (SECTIONS, D, D), ((0, 16), (1, 4), (2, 4)), -0.2, 0.2)), 1.990795135498047e-05, 0.00029945374).astype(jnp.bfloat16)
    cotangent = normal_values(splits[5], (SECTIONS, ROWS, D), 1.0, 6.0, ((0, 16), (1, 16)))
    preempted = draw_preempted(jax.random.fold_in(splits[7], 71), 0)
    return {"x_in": x_in, "gain": gain, "weight": weight, "moment_one": moment_one, "moment_two": moment_two, "cotangent": cotangent, "preempted": preempted}


EPSILON = 1e-05
BETA_ONE = 0.9
BETA_TWO = 0.95

def activate(values):
    return jax.nn.gelu(values, approximate=True)

def normalize(widened, gain_row):
    inverse = lax.rsqrt(lax.optimization_barrier(jnp.mean(widened * widened, axis=-1, keepdims=True)) + EPSILON)
    return widened * inverse * gain_row.astype(jnp.float32)

def layer_forward(inputs, gain_row, weight_full):
    widened = inputs.astype(jnp.float32)
    normed = normalize(widened, gain_row).astype(jnp.bfloat16)
    hidden = jnp.dot(normed, weight_full, preferred_element_type=jnp.float32)
    branch = activate(hidden).astype(jnp.bfloat16)
    output = (widened + branch.astype(jnp.float32)).astype(jnp.bfloat16)
    return (output, normed, hidden)

def layer_backward(incoming, inputs, gain_row, weight_full, hidden):
    upstream = incoming.astype(jnp.float32)
    hidden_grad = jax.vjp(activate, hidden)[1](upstream)[0].astype(jnp.bfloat16)
    normed_grad = lax.dot_general(hidden_grad, weight_full, (((1,), (1,)), ((), ())), preferred_element_type=jnp.float32)
    input_grad = jax.vjp(lambda values: normalize(values, gain_row), inputs.astype(jnp.float32))[1](normed_grad)[0]
    return (upstream + input_grad, hidden_grad)

def reference(x_in, gain, weight, moment_one, moment_two, cotangent, preempted):
    group_rows = TOK_DEV * N_TENSOR
    scale = 1.0 / (N_DP * group_rows)
    outputs = [[] for section in range(SECTIONS)]
    grads_in = [[] for section in range(SECTIONS)]
    saved = [[] for section in range(SECTIONS)]
    for group in range(N_DP):
        low = group * group_rows
        inputs = x_in[:, low:low + group_rows]
        upstream = cotangent[:, low:low + group_rows]
        flags = preempted[group] == 1
        first = [layer_forward(inputs[section], gain[section], weight[section]) for section in range(SECTIONS)]
        chosen = []
        for section in range(SECTIONS):
            previous = first[(section - 1) % SECTIONS][0]
            replay = layer_forward(previous, gain[section], weight[section])
            flag = flags[section]
            picked = tuple((jnp.where(flag, left, right) for left, right in zip(replay, first[section])))
            chosen.append((jnp.where(flag, previous, inputs[section]),) + picked)
        plain = []
        for section in range(SECTIONS):
            section_in, section_out, normed, hidden = chosen[section]
            early, unused = layer_backward(upstream[section], section_in, gain[section], weight[section], hidden)
            plain.append(early.astype(jnp.bfloat16))
        for section in range(SECTIONS):
            after = (section + 1) % SECTIONS
            summed = (upstream[section].astype(jnp.float32) + plain[after].astype(jnp.float32)).astype(jnp.bfloat16)
            incoming = jnp.where(flags[after], summed, upstream[section])
            section_in, section_out, normed, hidden = chosen[section]
            input_grad, hidden_grad = layer_backward(incoming, section_in, gain[section], weight[section], hidden)
            carried = input_grad.astype(jnp.bfloat16)
            outputs[section].append(section_out)
            grads_in[section].append(jnp.where(flags[section], jnp.zeros_like(carried), carried))
            saved[section].append((normed, hidden_grad))
    updates = []
    for section in range(SECTIONS):
        total = jnp.zeros((D, D), jnp.float32)
        for normed, hidden_grad in saved[section]:
            term = lax.dot_general(normed, hidden_grad, (((0,), (0,)), ((), ())), preferred_element_type=jnp.float32) * scale
            total = total + lax.optimization_barrier(term.astype(jnp.bfloat16)).astype(jnp.float32)
        first_moment = BETA_ONE * moment_one[section].astype(jnp.float32) + (1.0 - BETA_ONE) * total
        second_moment = BETA_TWO * moment_two[section].astype(jnp.float32) + (1.0 - BETA_TWO) * total * total
        updates.append((first_moment / (jnp.sqrt(second_moment) + 1e-08)).astype(jnp.bfloat16))
    y_out = jnp.stack([jnp.concatenate(outputs[section], axis=0) for section in range(SECTIONS)])
    dx_out = jnp.stack([jnp.concatenate(grads_in[section], axis=0) for section in range(SECTIONS)])
    return (y_out, dx_out, jnp.stack(updates))
```

```python
import jax
import jax.numpy as jnp
from jax import lax
from jax.sharding import PartitionSpec as P

EPSILON = 1e-05
BETA_ONE = 0.9
BETA_TWO = 0.95


def from_behind(value, axis, steps):
    count = lax.axis_size(axis)
    pairs = [(source, (source + steps) % count) for source in range(count)]
    return lax.ppermute(value, axis, pairs)


def activate(values):
    return jax.nn.gelu(values, approximate=True)


def normalize(widened, gain_row):
    inverse = lax.rsqrt(jnp.mean(widened * widened, axis=-1, keepdims=True) + EPSILON)
    return widened * inverse * gain_row.astype(jnp.float32)


def forward_part(inputs, gain_row, weight_cols):
    widened = inputs.astype(jnp.float32)
    normed_local = normalize(widened, gain_row).astype(jnp.bfloat16)
    normed_all = lax.all_gather(normed_local, "tensor", axis=0, tiled=True)
    hidden = jnp.dot(normed_all, weight_cols, preferred_element_type=jnp.float32)
    branch = activate(hidden).astype(jnp.bfloat16)
    branch_rows = lax.all_to_all(branch, "tensor", split_axis=0, concat_axis=1, tiled=True)
    output = (widened + branch_rows.astype(jnp.float32)).astype(jnp.bfloat16)
    return (output, normed_all, hidden)


def backward_part(incoming, inputs, gain_row, weight_cols, hidden):
    upstream = incoming.astype(jnp.float32)
    incoming_cols = lax.all_to_all(incoming, "tensor", split_axis=1, concat_axis=0, tiled=True)
    hidden_grad = jax.vjp(activate, hidden)[1](incoming_cols.astype(jnp.float32))[0].astype(
        jnp.bfloat16
    )
    normed_grad = lax.psum_scatter(
        lax.dot_general(
            hidden_grad, weight_cols, (((1,), (1,)), ((), ())), preferred_element_type=jnp.float32
        ).astype(jnp.bfloat16),
        "tensor",
        scatter_dimension=0,
        tiled=True,
    ).astype(jnp.float32)
    input_grad = jax.vjp(lambda values: normalize(values, gain_row), inputs.astype(jnp.float32))[1](
        normed_grad
    )[0]
    return (upstream + input_grad, hidden_grad)


def body(x_in, gain, weight, moment_one, moment_two, cotangent, preempted):
    section_here = lax.axis_index("section")
    section_count = lax.axis_size("section")
    group_here = lax.axis_index("dp")
    flag_row = lax.dynamic_index_in_dim(preempted, group_here, 0, keepdims=False)
    flag_self = lax.dynamic_index_in_dim(flag_row, section_here, 0, keepdims=False) == 1
    next_index = (section_here + 1) % section_count
    flag_next = lax.dynamic_index_in_dim(flag_row, next_index, 0, keepdims=False) == 1
    inputs = x_in[0]
    upstream = cotangent[0]
    gain_row = gain[0]
    weight_shard = weight[0]
    weight_cols = lax.all_gather(weight_shard, "dp", axis=0, tiled=True)
    first_out, _, _ = forward_part(inputs, gain_row, weight_cols)
    prior_rows = from_behind(first_out, "section", 1)
    section_in = jnp.where(flag_self, prior_rows, inputs)
    section_out, normed_all, hidden = forward_part(section_in, gain_row, weight_cols)
    early_grad, unused_grad = backward_part(upstream, section_in, gain_row, weight_cols, hidden)
    received = from_behind(early_grad.astype(jnp.bfloat16), "section", -1)
    summed = (upstream.astype(jnp.float32) + received.astype(jnp.float32)).astype(jnp.bfloat16)
    incoming = jnp.where(flag_next, summed, upstream)
    input_grad, hidden_grad = backward_part(incoming, section_in, gain_row, weight_cols, hidden)
    carried = input_grad.astype(jnp.bfloat16)
    grad_in = jnp.where(flag_self, jnp.zeros_like(carried), carried)
    scale = 1.0 / (lax.axis_size("dp") * inputs.shape[0] * lax.axis_size("tensor"))
    total = lax.psum_scatter(
        (
            lax.dot_general(
                normed_all,
                hidden_grad,
                (((0,), (0,)), ((), ())),
                preferred_element_type=jnp.float32,
            )
            * scale
        ).astype(jnp.bfloat16),
        "dp",
        scatter_dimension=0,
        tiled=True,
    ).astype(jnp.float32)
    first_moment = BETA_ONE * moment_one[0].astype(jnp.float32) + (1.0 - BETA_ONE) * total
    second_moment = BETA_TWO * moment_two[0].astype(jnp.float32) + (1.0 - BETA_TWO) * total * total
    step_dir = (first_moment / (jnp.sqrt(second_moment) + 1e-08)).astype(jnp.bfloat16)
    return (section_out[None], grad_in[None], step_dir[None])


def solution(mesh):
    placed = (
        P("section", ("dp", "tensor"), None),
        P("section", None),
        P("section", "dp", "tensor"),
        P("section", "dp", "tensor"),
        P("section", "dp", "tensor"),
        P("section", ("dp", "tensor"), None),
        P(),
    )
    return jax.shard_map(
        body,
        mesh=mesh,
        in_specs=placed,
        out_specs=(
            P("section", ("dp", "tensor"), None),
            P("section", ("dp", "tensor"), None),
            P("section", "dp", "tensor"),
        ),
        check_vma=False,
    )
```

```python
import functools

import jax
import jax.numpy as jnp
from jax import lax
from jax.experimental import pallas as pl
from jax.experimental.pallas import tpu as pltpu
from jax.sharding import PartitionSpec as P

EPSILON = 1e-05
BETA_ONE = 0.9
BETA_TWO = 0.95
GELU_SCALE = 0.7978845608028654
GELU_CUBE = 0.044715

D = 4096
CH = 4
ROWS = 128
SLAB = 32
COLS = 1024
TILE = 256
MESH = pl.DeviceIdType.MESH

(W_ANTI, W_FWD, W_SIB, X_ROWS, C_COLS, PRIOR_MOVE, GATHER_R, GATHER_L, RELAY_R, RELAY_L, Y_ONE, Y_TWO, Y_THREE,
 OPP_R, OPP_L, SUM_R, SUM_L, CARRY_MOVE, ROW_OPP_R, ROW_OPP_L, ROW_SUM_R, ROW_SUM_L, HG_SIB, HG_ANTI, HG_FWD,
 N_ANTI, N_SIB, N_R, N_L, N_RELAY_R, N_RELAY_L, N_SHARE) = range(32)


def gelu(v):
    return 0.5 * v * (1.0 + jnp.tanh(GELU_SCALE * (v + GELU_CUBE * v * v * v)))


def gelu_slope(v):
    square = v * v
    th = jnp.tanh(GELU_SCALE * v * (1.0 + GELU_CUBE * square))
    return 0.5 * (1.0 + th) + (0.5 * GELU_SCALE) * v * (1.0 - th * th) * (1.0 + 3.0 * GELU_CUBE * square)


def f32(v):
    return v.astype(jnp.float32)


def bf16(v):
    return v.astype(jnp.bfloat16)


def kernel(
    x_ref, cot_ref, w_ref, m1_ref, m2_ref, gain_ref, flag_ref,
    y_ref, dx_ref, upd_ref,
    w_all, x_all, in_all, nrm, hid, cot, prior, incoming, first_out, y_cols, carry,
    opp, to_r, to_l, own, got_a, got_b, got_l, got_r,
    part, row_a, row_b, row_l, row_r,
    hg, hg_sib, hg_anti, hg_other, hg_early, n_sib, n_anti, n_other, inv_s, dx_buf, m1_buf, m2_buf, upd_buf,
    send_sem, recv_sem, local_sem,
):
    t = lax.axis_index("tensor")
    d = lax.axis_index("dp")
    s = lax.axis_index("section")
    right, left, across = lax.rem(t + 1, 4), lax.rem(t + 3, 4), lax.rem(t + 2, 4)
    core = lax.rem(d, 2)
    half = d // 2
    sib = d + 1 - 2 * core
    anti = lax.rem(d + 2, 4)
    anti_sib = lax.rem(sib + 2, 4)
    after = lax.rem(s + 1, 16)
    before = lax.rem(s + 15, 16)
    to_right, to_left = {"tensor": right}, {"tensor": left}
    to_sib, to_anti = {"dp": sib}, {"dp": anti}
    to_after, to_before = {"section": after}, {"section": before}

    def cols(block):
        return pl.ds(pl.multiple_of(block * COLS, COLS), COLS)

    def tile(block, n):
        return pl.ds(pl.multiple_of(block * COLS + n * TILE, TILE), TILE)

    def copy(kind, index, src, dst, device):
        return pltpu.make_async_remote_copy(
            src_ref=src, dst_ref=dst, send_sem=send_sem.at[kind, index], recv_sem=recv_sem.at[kind, index],
            device_id=device, device_id_type=MESH,
        )

    def arrived(kind, index, where):
        copy(kind, index, where, where, to_sib).wait_recv()

    def sent(kind, index, where):
        copy(kind, index, where, where, to_sib).wait_send()

    barrier = pltpu.get_barrier_semaphore()
    for device in (to_right, to_left, {"tensor": across}, to_sib, to_anti, to_after, to_before):
        pl.semaphore_signal(barrier, inc=1, device_id=device, device_id_type=MESH)
    pl.semaphore_wait(barrier, 7)

    def rows_of(block, k):
        return pl.ds(pl.multiple_of(block * COLS + k * TILE, TILE), TILE)

    for k in range(4):
        copy(W_ANTI, k, w_ref.at[pl.ds(k * TILE, TILE)], w_all.at[rows_of(d, k)], to_anti).start()
    copy(W_SIB, 0, w_ref, w_all.at[cols(d)], to_sib).start()
    for k in range(1, 4):
        copy(X_ROWS, k - 1, x_ref, x_all.at[:, t], {"tensor": lax.rem(t + k, 4)}).start()
    loads = [
        pltpu.make_async_copy(x_ref, x_all.at[:, t], local_sem.at[0]),
        pltpu.make_async_copy(w_ref, w_all.at[cols(d)], local_sem.at[1]),
        pltpu.make_async_copy(cot_ref.at[:, :, cols(t)], cot.at[:, t], local_sem.at[2]),
        pltpu.make_async_copy(m1_ref, m1_buf, local_sem.at[3]),
        pltpu.make_async_copy(m2_ref, m2_buf, local_sem.at[4]),
    ]
    for load in loads:
        load.start()
    for k in range(1, 4):
        peer = lax.rem(t + k, 4)
        copy(C_COLS, k - 1, cot_ref.at[:, :, cols(peer)], cot.at[:, t], {"tensor": peer}).start()

    def normalize(read, j):
        def squares(b, total):
            u = read(pl.ds(pl.multiple_of(b * 512, 512), 512))
            u = u * u
            return total + (u[:, 0:128] + u[:, 128:256]) + (u[:, 256:384] + u[:, 384:512])

        total = lax.fori_loop(0, 8, squares, jnp.zeros((ROWS, 128), jnp.float32))
        inv = lax.rsqrt(jnp.sum(total, axis=-1, keepdims=True) * (1.0 / D) + EPSILON)

        def scale(b, _):
            where = pl.ds(pl.multiple_of(b * 512, 512), 512)
            nrm[j, :, :, where] = bf16(read(where) * inv * gain_ref[:, where]).reshape(4, SLAB, 512)
            return 0

        lax.fori_loop(0, 8, scale, 0)
        return inv

    loads[0].wait()
    for k in range(1, 4):
        arrived(X_ROWS, k - 1, x_all.at[:, lax.rem(t + 4 - k, 4)])

    def first_norm(j, _):
        normalize(lambda where: f32(x_all[j, :, :, where]).reshape(ROWS, -1), j)
        return 0

    lax.fori_loop(0, CH, first_norm, 0)

    def add_rows(block, k, clear=False):
        rows = rows_of(block, k)

        def step(n, _):
            there = pl.ds(pl.multiple_of(n * TILE, TILE), TILE)
            product = jnp.dot(
                nrm[:, :, :, rows].reshape(CH * ROWS, TILE), w_all[rows, there], preferred_element_type=jnp.float32
            ).reshape(CH, ROWS, TILE)
            if clear:
                hid[:, :, there] = product
            else:
                hid[:, :, there] += product
            return 0

        lax.fori_loop(0, 4, step, 0)

    loads[1].wait()
    add_rows(d, 0, clear=True)
    lax.fori_loop(1, 4, lambda k, _: (add_rows(d, k), 0)[1], 0)
    arrived(W_SIB, 0, w_all.at[cols(sib)])
    lax.fori_loop(0, 4, lambda k, _: (add_rows(sib, k), 0)[1], 0)
    loads[2].wait()
    for k in range(1, 4):
        arrived(C_COLS, k - 1, cot.at[:, lax.rem(t + 4 - k, 4)])

    def take(k, _):
        theirs = w_all.at[rows_of(anti, k)]
        arrived(W_ANTI, k, theirs)
        copy(W_FWD, k, theirs, theirs, to_sib).start()
        add_rows(anti, k)
        arrived(W_FWD, k, w_all.at[rows_of(anti_sib, k)])
        add_rows(anti_sib, k)
        return 0

    lax.fori_loop(0, 4, take, 0)

    def first_step(j, _):
        def step(n, _):
            there = pl.ds(pl.multiple_of(n * TILE, TILE), TILE)
            branch = f32(bf16(gelu(hid[j, :, there])))
            first_out[j, :, there] = bf16(f32(x_all[j, :, :, tile(t, n)]).reshape(ROWS, TILE) + branch)
            return 0

        lax.fori_loop(0, 4, step, 0)
        copy(PRIOR_MOVE, j, first_out.at[j], prior.at[j], to_after).start()
        return 0

    lax.fori_loop(0, CH, first_step, 0)

    def choose(j):
        arrived(PRIOR_MOVE, j, prior.at[j])

        def step(n, _):
            there = pl.ds(pl.multiple_of(n * TILE, TILE), TILE)
            mask = jnp.broadcast_to(flag_ref[0:1, 0:TILE], (ROWS, TILE)) > 0.5
            plain = f32(x_all[j, :, :, tile(t, n)]).reshape(ROWS, TILE)
            in_all[j, :, tile(t, n)] = bf16(jnp.where(mask, f32(prior[j, :, there]), plain))
            return 0

        lax.fori_loop(0, 4, step, 0)
        mine = in_all.at[j, :, cols(t)]
        copy(GATHER_R, j, mine, mine, to_right).start()
        copy(GATHER_L, j, mine, mine, to_left).start()

    def relay(j):
        arrived(GATHER_R, j, in_all.at[j, :, cols(left)])
        low = in_all.at[j, pl.ds(0, 64), cols(left)]
        copy(RELAY_R, j, low, low, to_right).start()
        arrived(GATHER_L, j, in_all.at[j, :, cols(right)])
        high = in_all.at[j, pl.ds(64, 64), cols(right)]
        copy(RELAY_L, j, high, high, to_left).start()

    def input_grad_tile(source, block, m, j, inv, slope):
        rows = tile(block, m)
        normed_grad = lax.dot_general(
            source, w_all[rows, :], (((1,), (1,)), ((), ())), preferred_element_type=jnp.float32
        )
        return normed_grad * (inv * gain_ref[:, rows]) - f32(in_all[j, :, rows]) * slope

    def forward(j):
        arrived(RELAY_R, j, in_all.at[j, pl.ds(0, 64), cols(across)])
        arrived(RELAY_L, j, in_all.at[j, pl.ds(64, 64), cols(across)])
        inv = normalize(lambda where: f32(in_all[j, :, where]), j)
        inv_s[j] = inv
        crossing = pl.ds(pl.multiple_of((1 - half) * 2048, 2048), 2048)
        copy(N_ANTI, j, nrm.at[j, t, :, crossing], n_anti.at[j, t], to_anti).start()
        copy(N_SIB, j, nrm.at[j, :, :, cols(sib)], n_sib.at[j], to_sib).start()

        def step(n, total):
            there = pl.ds(pl.multiple_of(n * TILE, TILE), TILE)
            hidden = jnp.dot(nrm[j].reshape(ROWS, D), w_all[:, there], preferred_element_type=jnp.float32)
            hid[j, :, there] = hidden
            branch = f32(bf16(gelu(hidden)))
            y_cols[j, :, :, there] = bf16(f32(in_all[j, :, tile(t, n)]) + branch).reshape(4, SLAB, TILE)
            upstream = f32(cot[j, :, :, there]).reshape(ROWS, TILE)
            grad = bf16(upstream * gelu_slope(hidden))
            hg_early[:, there] = grad
            return total + jnp.sum(f32(grad) * hidden, axis=-1, keepdims=True)

        total = lax.fori_loop(0, 4, step, jnp.zeros((ROWS, 1), jnp.float32))
        slope = inv * inv * total * (1.0 / D)

        def fill(target, block):
            def step(m, _):
                there = pl.ds(pl.multiple_of(m * TILE, TILE), TILE)
                target[j, :, there] = bf16(input_grad_tile(hg_early[...], block, m, j, inv, slope))
                return 0

            lax.fori_loop(0, 4, step, 0)

        fill(opp, across)
        copy(OPP_R, j, opp.at[j, pl.ds(0, 64)], got_a.at[j], to_right).start()
        copy(OPP_L, j, opp.at[j, pl.ds(64, 64)], got_b.at[j], to_left).start()
        fill(to_r, right)
        fill(to_l, left)
        fill(own, t)
        for k in range(1, 4):
            peer = lax.rem(t + k, 4)
            copy(Y_ONE + k - 1, j, y_cols.at[j, peer], y_ref.at[j, :, cols(t)], {"tensor": peer}).start()
        pltpu.make_async_copy(y_cols.at[j, t], y_ref.at[j, :, cols(t)], local_sem.at[5 + j]).start()

    def add_halves(j):
        arrived(OPP_R, j, got_a.at[j])
        to_r[j, 0:64, :] = bf16(f32(to_r[j, 0:64, :]) + f32(got_a[j]))
        copy(SUM_R, j, to_r.at[j], got_l.at[j], to_right).start()
        arrived(OPP_L, j, got_b.at[j])
        to_l[j, 64:128, :] = bf16(f32(to_l[j, 64:128, :]) + f32(got_b[j]))
        copy(SUM_L, j, to_l.at[j], got_r.at[j], to_left).start()

    def carry_on(j):
        arrived(SUM_R, j, got_l.at[j])
        arrived(SUM_L, j, got_r.at[j])

        def step(n, _):
            there = pl.ds(pl.multiple_of(n * TILE, TILE), TILE)
            total = (f32(got_l[j, :, there]) + f32(got_r[j, :, there])) + f32(own[j, :, there])
            carry[j, :, there] = bf16(f32(cot[j, :, :, there]).reshape(ROWS, TILE) + total)
            return 0

        lax.fori_loop(0, 4, step, 0)
        copy(CARRY_MOVE, j, carry.at[j], incoming.at[j], to_before).start()

    def backward(j):
        arrived(CARRY_MOVE, j, incoming.at[j])

        def step(n, total):
            there = pl.ds(pl.multiple_of(n * TILE, TILE), TILE)
            mask = jnp.broadcast_to(flag_ref[1:2, 0:TILE], (ROWS, TILE)) > 0.5
            upstream = f32(cot[j, :, :, there]).reshape(ROWS, TILE)
            summed = bf16(upstream + jnp.where(mask, f32(incoming[j, :, there]), 0.0))
            incoming[j, :, there] = summed
            hidden = hid[j, :, there]
            grad = bf16(f32(summed) * gelu_slope(hidden))
            hg[j, :, there] = grad
            return total + jnp.sum(f32(grad) * hidden, axis=-1, keepdims=True)

        total = lax.fori_loop(0, 4, step, jnp.zeros((ROWS, 1), jnp.float32))
        copy(HG_ANTI, j, hg.at[j], hg_anti.at[j], to_anti).start()
        copy(HG_SIB, j, hg.at[j], hg_sib.at[j], to_sib).start()
        inv = inv_s[j]
        slope = inv * inv * total * (1.0 / D)

        def other(q, _):
            block = lax.rem(t + 1 + q // 4, 4)
            m = lax.rem(q, 4)
            value = bf16(input_grad_tile(hg[j], block, m, j, inv, slope))
            part[j, :, :, tile(block, m)] = value.reshape(4, SLAB, TILE)
            return 0

        lax.fori_loop(0, 12, other, 0)

        def mine(m, _):
            there = pl.ds(pl.multiple_of(m * TILE, TILE), TILE)
            value = input_grad_tile(hg[j], t, m, j, inv, slope) + f32(incoming[j, :, there])
            part[j, :, :, tile(t, m)] = bf16(value).reshape(4, SLAB, TILE)
            return 0

        lax.fori_loop(0, 4, mine, 0)
        copy(ROW_OPP_R, j, part.at[j, across, pl.ds(0, 16)], row_a.at[j], to_right).start()
        copy(ROW_OPP_L, j, part.at[j, across, pl.ds(16, 16)], row_b.at[j], to_left).start()

    def add_row_halves(j):
        arrived(ROW_OPP_R, j, row_a.at[j])
        part[j, right, 0:16, :] = bf16(f32(part[j, right, 0:16, :]) + f32(row_a[j]))
        copy(ROW_SUM_R, j, part.at[j, right], row_l.at[j], to_right).start()
        arrived(ROW_OPP_L, j, row_b.at[j])
        part[j, left, 16:32, :] = bf16(f32(part[j, left, 16:32, :]) + f32(row_b[j]))
        copy(ROW_SUM_L, j, part.at[j, left], row_r.at[j], to_left).start()

    def finish_rows(j):
        arrived(ROW_SUM_R, j, row_l.at[j])
        arrived(ROW_SUM_L, j, row_r.at[j])

        def step(b, _):
            there = pl.ds(pl.multiple_of(b * 1024, 1024), 1024)
            total = (f32(row_l[j, :, there]) + f32(row_r[j, :, there])) + f32(part[j, t, :, there])
            mask = jnp.broadcast_to(flag_ref[0:1, 0:1024], (SLAB, 1024)) > 0.5
            dx_buf[j, :, there] = bf16(jnp.where(mask, 0.0, total))
            return 0

        lax.fori_loop(0, 4, step, 0)
        pltpu.make_async_copy(dx_buf.at[j], dx_ref.at[j], local_sem.at[9 + j]).start()

    def spread_normed(j):
        arrived(N_ANTI, j, n_anti.at[j, t])
        copy(N_R, j, n_anti.at[j, t], n_anti.at[j, t], to_right).start()
        copy(N_L, j, n_anti.at[j, t], n_anti.at[j, t], to_left).start()

    def relay_normed(j):
        arrived(N_R, j, n_anti.at[j, left])
        low = n_anti.at[j, left, pl.ds(0, 16)]
        copy(N_RELAY_R, j, low, low, to_right).start()
        arrived(N_L, j, n_anti.at[j, right])
        high = n_anti.at[j, right, pl.ds(16, 16)]
        copy(N_RELAY_L, j, high, high, to_left).start()

    def share_normed(j):
        arrived(N_RELAY_R, j, n_anti.at[j, across, pl.ds(0, 16)])
        arrived(N_RELAY_L, j, n_anti.at[j, across, pl.ds(16, 16)])
        theirs = pl.ds(pl.multiple_of((1 - core) * COLS, COLS), COLS)
        copy(N_SHARE, j, n_anti.at[j, :, :, theirs], n_other.at[j], to_sib).start()

    def pass_grad(j):
        arrived(HG_ANTI, j, hg_anti.at[j])
        copy(HG_FWD, j, hg_anti.at[j], hg_other.at[j], to_sib).start()

    def stage(run, j):
        pl.when(jnp.logical_and(j >= 0, j < CH))(lambda: run(j))

    def turn(i, _):
        stage(choose, i)
        stage(add_halves, i - 1)
        stage(backward, i - 2)
        stage(relay, i)
        stage(spread_normed, i - 1)
        stage(add_row_halves, i - 2)
        stage(carry_on, i - 1)
        stage(relay_normed, i - 2)
        stage(finish_rows, i - 3)
        stage(pass_grad, i - 3)
        stage(share_normed, i - 3)
        stage(forward, i)
        return 0

    lax.fori_loop(0, CH + 3, turn, 0)

    def last_arrivals(j, _):
        arrived(HG_SIB, j, hg_sib.at[j])
        arrived(HG_FWD, j, hg_other.at[j])
        arrived(N_SIB, j, n_sib.at[j])
        arrived(N_SHARE, j, n_other.at[j])
        return 0

    lax.fori_loop(0, CH, last_arrivals, 0)
    loads[3].wait()
    loads[4].wait()

    def product(left_rows, right_rows):
        return lax.dot_general(
            left_rows.reshape(CH * ROWS, TILE), right_rows.reshape(CH * ROWS, 512),
            (((0,), (0,)), ((), ())), preferred_element_type=jnp.float32,
        )

    def step_dir(q, _):
        f = q // 2
        rows = pl.ds(pl.multiple_of(f * TILE, TILE), TILE)
        there = pl.ds(pl.multiple_of(lax.rem(q, 2) * 512, 512), 512)
        total = product(nrm[:, :, :, tile(d, f)], hg[:, :, there])
        total += product(n_sib[:, :, :, rows], hg_sib[:, :, there])
        total += product(n_anti[:, :, :, tile(core, f)], hg_anti[:, :, there])
        total += product(n_other[:, :, :, rows], hg_other[:, :, there])
        total = total * (1.0 / (4 * CH * ROWS))
        first = BETA_ONE * f32(m1_buf[rows, there]) + (1.0 - BETA_ONE) * total
        second = BETA_TWO * f32(m2_buf[rows, there]) + (1.0 - BETA_TWO) * total * total
        upd_buf[rows, there] = bf16(first / (jnp.sqrt(second) + 1e-08))
        return 0

    lax.fori_loop(0, 8, step_dir, 0)
    out = pltpu.make_async_copy(upd_buf, upd_ref, local_sem.at[13])
    out.start()

    def drain(j, _):
        for k in range(1, 4):
            arrived(Y_ONE + k - 1, j, y_ref.at[j, :, cols(lax.rem(t + 4 - k, 4))])
            sent(Y_ONE + k - 1, j, y_cols.at[j, 0])
        pltpu.make_async_copy(y_cols.at[j, t], y_ref.at[j, :, cols(t)], local_sem.at[5 + j]).wait()
        pltpu.make_async_copy(dx_buf.at[j], dx_ref.at[j], local_sem.at[9 + j]).wait()
        sent(W_ANTI, j, w_all.at[rows_of(d, 0)])
        sent(W_FWD, j, w_all.at[rows_of(anti, j)])
        sent(PRIOR_MOVE, j, first_out.at[j])
        sent(GATHER_R, j, in_all.at[j, :, cols(t)])
        sent(GATHER_L, j, in_all.at[j, :, cols(t)])
        sent(RELAY_R, j, in_all.at[j, pl.ds(0, 64), cols(left)])
        sent(RELAY_L, j, in_all.at[j, pl.ds(64, 64), cols(right)])
        sent(OPP_R, j, opp.at[j, pl.ds(0, 64)])
        sent(OPP_L, j, opp.at[j, pl.ds(64, 64)])
        sent(SUM_R, j, to_r.at[j])
        sent(SUM_L, j, to_l.at[j])
        sent(CARRY_MOVE, j, carry.at[j])
        sent(ROW_OPP_R, j, part.at[j, across, pl.ds(0, 16)])
        sent(ROW_OPP_L, j, part.at[j, across, pl.ds(16, 16)])
        sent(ROW_SUM_R, j, part.at[j, right])
        sent(ROW_SUM_L, j, part.at[j, left])
        sent(HG_SIB, j, hg.at[j])
        sent(HG_ANTI, j, hg.at[j])
        sent(HG_FWD, j, hg_anti.at[j])
        sent(N_ANTI, j, n_anti.at[j, t])
        sent(N_SIB, j, n_sib.at[j])
        sent(N_R, j, n_anti.at[j, t])
        sent(N_L, j, n_anti.at[j, t])
        sent(N_RELAY_R, j, n_anti.at[j, left, pl.ds(0, 16)])
        sent(N_RELAY_L, j, n_anti.at[j, right, pl.ds(16, 16)])
        sent(N_SHARE, j, n_other.at[j])
        return 0

    lax.fori_loop(0, CH, drain, 0)
    sent(W_SIB, 0, w_all.at[cols(d)])
    for k in range(3):
        sent(X_ROWS, k, x_all.at[:, t])
        sent(C_COLS, k, cot.at[:, t])
    out.wait()


def whole(x, cot, w, m1, m2, gain, flags):
    def vm(*shape, dtype=jnp.bfloat16):
        return pltpu.VMEM(shape, dtype)

    scratch = [
        vm(D, COLS), vm(CH, 4, SLAB, D), vm(CH, ROWS, D), vm(CH, 4, SLAB, D),
        vm(CH, ROWS, COLS, dtype=jnp.float32), vm(CH, 4, SLAB, COLS),
        vm(CH, ROWS, COLS), vm(CH, ROWS, COLS), vm(CH, ROWS, COLS), vm(CH, 4, SLAB, COLS), vm(CH, ROWS, COLS),
        vm(CH, ROWS, COLS), vm(CH, ROWS, COLS), vm(CH, ROWS, COLS), vm(CH, ROWS, COLS),
        vm(CH, 64, COLS), vm(CH, 64, COLS), vm(CH, ROWS, COLS), vm(CH, ROWS, COLS),
        vm(CH, 4, SLAB, D), vm(CH, 16, D), vm(CH, 16, D), vm(CH, SLAB, D), vm(CH, SLAB, D),
        vm(CH, ROWS, COLS), vm(CH, ROWS, COLS), vm(CH, ROWS, COLS), vm(CH, ROWS, COLS), vm(ROWS, COLS),
        vm(CH, 4, SLAB, COLS), vm(CH, 4, SLAB, 2 * COLS), vm(CH, 4, SLAB, COLS),
        vm(CH, ROWS, 1, dtype=jnp.float32), vm(CH, SLAB, D), vm(COLS, COLS), vm(COLS, COLS), vm(COLS, COLS),
        pltpu.SemaphoreType.DMA((32, CH)), pltpu.SemaphoreType.DMA((32, CH)), pltpu.SemaphoreType.DMA((14,)),
    ]
    anywhere = pl.BlockSpec(memory_space=pl.ANY)
    near = pl.BlockSpec(memory_space=pltpu.VMEM)
    return pl.pallas_call(
        kernel,
        out_shape=(
            jax.ShapeDtypeStruct((CH, SLAB, D), jnp.bfloat16),
            jax.ShapeDtypeStruct((CH, SLAB, D), jnp.bfloat16),
            jax.ShapeDtypeStruct((COLS, COLS), jnp.bfloat16),
        ),
        in_specs=[anywhere] * 5 + [near] * 2,
        out_specs=(anywhere,) * 3,
        scratch_shapes=scratch,
        compiler_params=pltpu.CompilerParams(
            collective_id=0, has_side_effects=True, vmem_limit_bytes=63 * 2**20
        ),
        cost_estimate=pl.CostEstimate(flops=21 * 10**9, bytes_accessed=20 * 2**20, transcendentals=2 * 10**6),
    )(x, cot, w, m1, m2, gain, flags)


def body(x_in, gain, weight, moment_one, moment_two, cotangent, preempted):
    section_here = lax.axis_index("section")
    flag_row = lax.dynamic_index_in_dim(preempted, lax.axis_index("dp"), 0, keepdims=False)
    flag_self = lax.dynamic_index_in_dim(flag_row, section_here, 0, keepdims=False)
    flag_next = lax.dynamic_index_in_dim(flag_row, (section_here + 1) % 16, 0, keepdims=False)
    flags = jnp.stack([flag_self, flag_next]).astype(jnp.float32)
    flags = jnp.broadcast_to(flags[:, None], (2, COLS))
    y, dx, update = whole(
        x_in.reshape(CH, SLAB, D), cotangent.reshape(CH, SLAB, D), weight[0], moment_one[0], moment_two[0],
        gain.astype(jnp.float32), flags,
    )
    return (y.reshape(1, CH * SLAB, D), dx.reshape(1, CH * SLAB, D), update[None])


def solution(mesh):
    placed = (
        P("section", ("dp", "tensor"), None),
        P("section", None),
        P("section", "dp", "tensor"),
        P("section", "dp", "tensor"),
        P("section", "dp", "tensor"),
        P("section", ("dp", "tensor"), None),
        P(),
    )
    return jax.shard_map(
        body,
        mesh=mesh,
        in_specs=placed,
        out_specs=(
            P("section", ("dp", "tensor"), None),
            P("section", ("dp", "tensor"), None),
            P("section", "dp", "tensor"),
        ),
        check_vma=False,
    )
```

```python
import jax
import jax.numpy as jnp
from jax import lax
from jax.experimental import pallas as pl
from jax.experimental.pallas import tpu as pltpu
from jax.sharding import PartitionSpec as P

EPSILON = 1e-05
BETA_ONE = 0.9
BETA_TWO = 0.95
GELU_SCALE = 0.7978845608028654
GELU_CUBE = 0.044715

D = 4096
CH = 4
ROWS = 128
SLAB = 32
COLS = 1024
TILE = 256
MESH = pl.DeviceIdType.MESH

(W_ANTI, W_FWD, W_SIB, X_ONE, X_TWO, X_THREE, C_COLS, PRIOR_MOVE, GATHER_R, GATHER_L, RELAY_R, RELAY_L,
 Y_ONE, Y_TWO, Y_THREE,
 OPP_R, OPP_L, SUM_R, SUM_L, CARRY_MOVE, ROW_OPP_R, ROW_OPP_L, ROW_SUM_R, ROW_SUM_L, HG_SIB, HG_ANTI, HG_FWD,
 N_ANTI, N_SIB, N_R, N_L, N_RELAY_R, N_RELAY_L, N_SHARE) = range(34)


def gelu(v):
    return 0.5 * v * (1.0 + jnp.tanh(GELU_SCALE * (v + GELU_CUBE * v * v * v)))


def gelu_slope(v):
    square = v * v
    th = jnp.tanh(GELU_SCALE * v * (1.0 + GELU_CUBE * square))
    return 0.5 * (1.0 + th) + (0.5 * GELU_SCALE) * v * (1.0 - th * th) * (1.0 + 3.0 * GELU_CUBE * square)


def f32(v):
    return v.astype(jnp.float32)


def bf16(v):
    return v.astype(jnp.bfloat16)


def kernel(
    x_ref, cot_ref, w_ref, m1_ref, m2_ref, gain_ref, flag_ref,
    y_ref, dx_ref, upd_ref,
    w_all, w_t, x_all, in_all, nrm, hid, cot, prior, incoming, y_cols,
    opp, to_r, to_l, own, got_a, got_b, got_l, got_r,
    part, row_a, row_b, row_l, row_r,
    hg, hg_sib, hg_anti, hg_other, n_sib, n_anti, n_other, inv_s, total_s,
    send_sem, recv_sem, local_sem,
):
    t = lax.axis_index("tensor")
    d = lax.axis_index("dp")
    s = lax.axis_index("section")
    right, left, across = lax.rem(t + 1, 4), lax.rem(t + 3, 4), lax.rem(t + 2, 4)
    core = lax.rem(d, 2)
    half = d // 2
    sib = d + 1 - 2 * core
    anti = lax.rem(d + 2, 4)
    anti_sib = lax.rem(sib + 2, 4)
    after = lax.rem(s + 1, 16)
    before = lax.rem(s + 15, 16)
    to_right, to_left = {"tensor": right}, {"tensor": left}
    to_sib, to_anti = {"dp": sib}, {"dp": anti}
    to_after, to_before = {"section": after}, {"section": before}

    def cols(block):
        return pl.ds(pl.multiple_of(block * COLS, COLS), COLS)

    def tile(block, n):
        return pl.ds(pl.multiple_of(block * COLS + n * TILE, TILE), TILE)

    def copy(kind, index, src, dst, device):
        return pltpu.make_async_remote_copy(
            src_ref=src, dst_ref=dst, send_sem=send_sem.at[kind, index], recv_sem=recv_sem.at[kind, index],
            device_id=device, device_id_type=MESH,
        )

    def arrived(kind, index, where):
        copy(kind, index, where, where, to_sib).wait_recv()

    def sent(kind, index, where):
        copy(kind, index, where, where, to_sib).wait_send()

    barrier = pltpu.get_barrier_semaphore()
    for device in (to_right, to_left, {"tensor": across}, to_sib, to_anti, to_after, to_before):
        pl.semaphore_signal(barrier, inc=1, device_id=device, device_id_type=MESH)
    pl.semaphore_wait(barrier, 7)

    flag_self = flag_ref[d, s]
    flag_next = flag_ref[d, after]

    def quarter(k):
        return pl.ds(pl.multiple_of(k * TILE, TILE), TILE)

    for k in range(4):
        copy(W_ANTI, k, w_ref.at[:, quarter(k)], w_all.at[cols(d), quarter(k)], to_anti).start()
    copy(W_SIB, 0, w_ref, w_all.at[cols(d)], to_sib).start()
    for b in range(4):
        for k in range(1, 4):
            copy(
                X_ONE + k - 1, b, x_ref.at[:, :, cols(b)], x_all.at[b, :, t], {"tensor": lax.rem(t + k, 4)}
            ).start()
    loads = [pltpu.make_async_copy(x_ref.at[:, :, cols(b)], x_all.at[b, :, t], local_sem.at[b]) for b in range(4)]
    loads += [
        pltpu.make_async_copy(w_ref, w_all.at[cols(d)], local_sem.at[4]),
        pltpu.make_async_copy(cot_ref.at[:, :, cols(t)], cot.at[:, t], local_sem.at[5]),
    ]
    for load in loads:
        load.start()
    for k in range(1, 4):
        peer = lax.rem(t + k, 4)
        copy(C_COLS, k - 1, cot_ref.at[:, :, cols(peer)], cot.at[:, t], {"tensor": peer}).start()

    def normalize(read, j):
        def squares(b, total):
            u = read(b)
            u = u * u
            return total + (u[:, 0:128] + u[:, 128:256]) + (u[:, 256:384] + u[:, 384:512])

        total = lax.fori_loop(0, 8, squares, jnp.zeros((ROWS, 128), jnp.float32))
        inv = lax.rsqrt(jnp.sum(total, axis=-1, keepdims=True) * (1.0 / D) + EPSILON)

        def scale(b, _):
            where = pl.ds(pl.multiple_of(b * 512, 512), 512)
            nrm[j, :, :, where] = bf16(read(b) * inv * f32(gain_ref[:, where])).reshape(4, SLAB, 512)
            return 0

        lax.fori_loop(0, 8, scale, 0)
        return inv

    for b in range(4):
        loads[b].wait()
        for k in range(1, 4):
            arrived(X_ONE + k - 1, b, x_all.at[b, :, lax.rem(t + 4 - k, 4)])

    def first_norm(j, _):
        def read(b):
            where = pl.ds(pl.multiple_of(lax.rem(b, 2) * 512, 512), 512)
            return f32(x_all[b // 2, j, :, :, where]).reshape(ROWS, 512)

        normalize(read, j)
        return 0

    lax.fori_loop(0, CH, first_norm, 0)
    loads[4].wait()
    arrived(W_SIB, 0, w_all.at[cols(sib)])

    def add_rows(block, k, clear=False):
        there = quarter(k)
        product = jnp.dot(
            nrm[:, :, :, cols(block)].reshape(CH * ROWS, COLS), w_all[cols(block), there],
            preferred_element_type=jnp.float32,
        ).reshape(CH, ROWS, TILE)
        if clear:
            hid[:, :, there] = product
        else:
            hid[:, :, there] += product

    def turn_weight(k):
        def step(m, _):
            w_t[quarter(k), quarter(m)] = w_all[quarter(m), quarter(k)].T
            return 0

        lax.fori_loop(0, 16, step, 0)

    def first_tile(j, k):
        there = quarter(k)
        branch = f32(bf16(gelu(hid[j, :, there])))
        value = bf16(f32(x_all[t, j, :, :, there]).reshape(ROWS, TILE) + branch)
        y_cols[j, :, :, there] = value.reshape(4, SLAB, TILE)

    def take(k, _):
        add_rows(d, k, clear=True)
        add_rows(sib, k)
        theirs = w_all.at[cols(anti), quarter(k)]
        arrived(W_ANTI, k, theirs)
        copy(W_FWD, k, theirs, theirs, to_sib).start()
        add_rows(anti, k)
        arrived(W_FWD, k, w_all.at[cols(anti_sib), quarter(k)])
        add_rows(anti_sib, k)

        lax.fori_loop(0, CH, lambda j, _: (first_tile(j, k), 0)[1], 0)
        turn_weight(k)
        return 0

    def take_last(k):
        add_rows(d, k, clear=True)
        add_rows(sib, k)
        theirs = w_all.at[cols(anti), quarter(k)]
        arrived(W_ANTI, k, theirs)
        copy(W_FWD, k, theirs, theirs, to_sib).start()
        add_rows(anti, k)
        arrived(W_FWD, k, w_all.at[cols(anti_sib), quarter(k)])
        add_rows(anti_sib, k)

        def step(j, _):
            first_tile(j, k)
            copy(PRIOR_MOVE, j, y_cols.at[j], prior.at[j], to_after).start()
            return 0

        lax.fori_loop(0, CH, step, 0)
        turn_weight(k)

    lax.fori_loop(0, 3, take, 0)
    take_last(3)
    loads[5].wait()
    for k in range(1, 4):
        arrived(C_COLS, k - 1, cot.at[:, lax.rem(t + 4 - k, 4)])

    moments = [
        pltpu.make_async_copy(m1_ref, x_all.at[0:2], local_sem.at[0]),
        pltpu.make_async_copy(m2_ref, x_all.at[2:4], local_sem.at[1]),
    ]

    def choose(j):
        arrived(PRIOR_MOVE, j, prior.at[j])

        def step(n, _):
            there = quarter(n)
            mask = jnp.full((ROWS, TILE), flag_self, jnp.int32) == 1
            plain = f32(x_all[t, j, :, :, there]).reshape(ROWS, TILE)
            in_all[j, :, tile(t, n)] = bf16(jnp.where(mask, f32(prior[j, :, :, there]).reshape(ROWS, TILE), plain))
            return 0

        lax.fori_loop(0, 4, step, 0)
        mine = in_all.at[j, :, cols(t)]
        copy(GATHER_R, j, mine, mine, to_right).start()
        copy(GATHER_L, j, mine, mine, to_left).start()

        @pl.when(j == CH - 1)
        def _():
            for load in moments:
                load.start()

    def relay(j):
        arrived(GATHER_R, j, in_all.at[j, :, cols(left)])
        low = in_all.at[j, pl.ds(0, 64), cols(left)]
        copy(RELAY_R, j, low, low, to_right).start()
        arrived(GATHER_L, j, in_all.at[j, :, cols(right)])
        high = in_all.at[j, pl.ds(64, 64), cols(right)]
        copy(RELAY_L, j, high, high, to_left).start()

    def input_grad_tile(source, block, m, j, inv, slope):
        rows = tile(block, m)
        normed_grad = jnp.dot(source, w_t[:, rows], preferred_element_type=jnp.float32)
        return normed_grad * (inv * f32(gain_ref[:, rows])) - f32(in_all[j, :, rows]) * slope

    def forward(j):
        arrived(RELAY_R, j, in_all.at[j, pl.ds(0, 64), cols(across)])
        arrived(RELAY_L, j, in_all.at[j, pl.ds(64, 64), cols(across)])
        sent(PRIOR_MOVE, j, y_cols.at[j])
        inv = normalize(lambda b: f32(in_all[j, :, pl.ds(pl.multiple_of(b * 512, 512), 512)]), j)
        inv_s[j] = inv
        crossing = pl.ds(pl.multiple_of((1 - half) * 2048, 2048), 2048)
        copy(N_ANTI, j, nrm.at[j, t, :, crossing], n_anti.at[j, t], to_anti).start()
        copy(N_SIB, j, nrm.at[j, :, :, cols(sib)], n_sib.at[j], to_sib).start()

        def step(n, total):
            there = pl.ds(pl.multiple_of(n * TILE, TILE), TILE)
            hidden = jnp.dot(nrm[j].reshape(ROWS, D), w_all[:, there], preferred_element_type=jnp.float32)
            hid[j, :, there] = hidden
            branch = f32(bf16(gelu(hidden)))
            y_cols[j, :, :, there] = bf16(f32(in_all[j, :, tile(t, n)]) + branch).reshape(4, SLAB, TILE)
            upstream = f32(cot[j, :, :, there]).reshape(ROWS, TILE)
            grad = bf16(upstream * gelu_slope(hidden))
            hg[j, :, there] = grad
            return total + jnp.sum(f32(grad) * hidden, axis=-1, keepdims=True)

        total_s[j] = lax.fori_loop(0, 4, step, jnp.zeros((ROWS, 1), jnp.float32))

    def fill(target, block, j):
        inv = inv_s[j]
        slope = inv * inv * total_s[j] * (1.0 / D)

        def step(m, _):
            value = bf16(input_grad_tile(hg[j], block, m, j, inv, slope))
            target[j, :, quarter(m)] = value
            return 0

        lax.fori_loop(0, 4, step, 0)

    def far_sum(j):
        fill(opp, across, j)
        copy(OPP_R, j, opp.at[j, pl.ds(0, 64)], got_a.at[j], to_right).start()
        copy(OPP_L, j, opp.at[j, pl.ds(64, 64)], got_b.at[j], to_left).start()

    def near_sums(j):
        fill(to_r, right, j)
        fill(to_l, left, j)
        fill(own, t, j)

    def give_rows(j):
        for k in range(1, 4):
            peer = lax.rem(t + k, 4)
            copy(Y_ONE + k - 1, j, y_cols.at[j, peer], y_ref.at[j, :, cols(t)], {"tensor": peer}).start()
        pltpu.make_async_copy(y_cols.at[j, t], y_ref.at[j, :, cols(t)], local_sem.at[6 + j]).start()

    def add_halves(j):
        arrived(OPP_R, j, got_a.at[j])
        to_r[j, 0:64, :] = bf16(f32(to_r[j, 0:64, :]) + f32(got_a[j]))
        copy(SUM_R, j, to_r.at[j], got_l.at[j], to_right).start()
        arrived(OPP_L, j, got_b.at[j])
        to_l[j, 64:128, :] = bf16(f32(to_l[j, 64:128, :]) + f32(got_b[j]))
        copy(SUM_L, j, to_l.at[j], got_r.at[j], to_left).start()

    def carry_on(j):
        arrived(SUM_R, j, got_l.at[j])
        arrived(SUM_L, j, got_r.at[j])

        def step(n, _):
            there = pl.ds(pl.multiple_of(n * TILE, TILE), TILE)
            total = (f32(got_l[j, :, there]) + f32(got_r[j, :, there])) + f32(own[j, :, there])
            own[j, :, there] = bf16(f32(cot[j, :, :, there]).reshape(ROWS, TILE) + total)
            return 0

        lax.fori_loop(0, 4, step, 0)
        copy(CARRY_MOVE, j, own.at[j], incoming.at[j], to_before).start()

    def backward(j):
        arrived(CARRY_MOVE, j, incoming.at[j])

        def step(n, total):
            there = pl.ds(pl.multiple_of(n * TILE, TILE), TILE)
            mask = jnp.full((ROWS, TILE), flag_next, jnp.int32) == 1
            upstream = f32(cot[j, :, :, there]).reshape(ROWS, TILE)
            summed = bf16(upstream + jnp.where(mask, f32(incoming[j, :, there]), 0.0))
            incoming[j, :, there] = summed
            hidden = hid[j, :, there]
            grad = bf16(f32(summed) * gelu_slope(hidden))
            hg[j, :, there] = grad
            return total + jnp.sum(f32(grad) * hidden, axis=-1, keepdims=True)

        total_s[j] = lax.fori_loop(0, 4, step, jnp.zeros((ROWS, 1), jnp.float32))
        copy(HG_ANTI, j, hg.at[j], hg_anti.at[j], to_anti).start()
        copy(HG_SIB, j, hg.at[j], hg_sib.at[j], to_sib).start()

    def row_sums(j):
        inv = inv_s[j]
        slope = inv * inv * total_s[j] * (1.0 / D)

        def other(q, _):
            block = lax.rem(t + 1 + q // 4, 4)
            m = lax.rem(q, 4)
            value = bf16(input_grad_tile(hg[j], block, m, j, inv, slope))
            part[j, :, :, tile(block, m)] = value.reshape(4, SLAB, TILE)
            return 0

        lax.fori_loop(0, 12, other, 0)

        def mine(m, _):
            there = pl.ds(pl.multiple_of(m * TILE, TILE), TILE)
            value = input_grad_tile(hg[j], t, m, j, inv, slope) + f32(incoming[j, :, there])
            part[j, :, :, tile(t, m)] = bf16(value).reshape(4, SLAB, TILE)
            return 0

        lax.fori_loop(0, 4, mine, 0)
        copy(ROW_OPP_R, j, part.at[j, across, pl.ds(0, 16)], row_a.at[j], to_right).start()
        copy(ROW_OPP_L, j, part.at[j, across, pl.ds(16, 16)], row_b.at[j], to_left).start()

    def add_row_halves(j):
        arrived(ROW_OPP_R, j, row_a.at[j])
        part[j, right, 0:16, :] = bf16(f32(part[j, right, 0:16, :]) + f32(row_a[j]))
        copy(ROW_SUM_R, j, part.at[j, right], row_l.at[j], to_right).start()
        arrived(ROW_OPP_L, j, row_b.at[j])
        part[j, left, 16:32, :] = bf16(f32(part[j, left, 16:32, :]) + f32(row_b[j]))
        copy(ROW_SUM_L, j, part.at[j, left], row_r.at[j], to_left).start()

    def finish_rows(j):
        arrived(ROW_SUM_R, j, row_l.at[j])
        arrived(ROW_SUM_L, j, row_r.at[j])

        def step(b, _):
            there = pl.ds(pl.multiple_of(b * 1024, 1024), 1024)
            total = (f32(row_l[j, :, there]) + f32(row_r[j, :, there])) + f32(part[j, t, :, there])
            mask = jnp.full((SLAB, 1024), flag_self, jnp.int32) == 1
            row_l[j, :, there] = bf16(jnp.where(mask, 0.0, total))
            return 0

        lax.fori_loop(0, 4, step, 0)
        pltpu.make_async_copy(row_l.at[j], dx_ref.at[j], local_sem.at[10 + j]).start()

    def spread_normed(j):
        arrived(N_ANTI, j, n_anti.at[j, t])
        copy(N_R, j, n_anti.at[j, t], n_anti.at[j, t], to_right).start()
        copy(N_L, j, n_anti.at[j, t], n_anti.at[j, t], to_left).start()

    def relay_normed(j):
        arrived(N_R, j, n_anti.at[j, left])
        low = n_anti.at[j, left, pl.ds(0, 16)]
        copy(N_RELAY_R, j, low, low, to_right).start()
        arrived(N_L, j, n_anti.at[j, right])
        high = n_anti.at[j, right, pl.ds(16, 16)]
        copy(N_RELAY_L, j, high, high, to_left).start()

    def share_normed(j):
        arrived(N_RELAY_R, j, n_anti.at[j, across, pl.ds(0, 16)])
        arrived(N_RELAY_L, j, n_anti.at[j, across, pl.ds(16, 16)])
        theirs = pl.ds(pl.multiple_of((1 - core) * COLS, COLS), COLS)
        copy(N_SHARE, j, n_anti.at[j, :, :, theirs], n_other.at[j], to_sib).start()

    def pass_grad(j):
        arrived(HG_ANTI, j, hg_anti.at[j])
        copy(HG_FWD, j, hg_anti.at[j], hg_other.at[j], to_sib).start()

    def stage(run, j):
        pl.when(jnp.logical_and(j >= 0, j < CH))(lambda: run(j))

    def turn(i, _):
        stage(relay_normed, i - 4)
        stage(choose, i)
        stage(near_sums, i - 3)
        stage(share_normed, i - 6)
        stage(relay, i - 1)
        stage(forward, i - 2)
        stage(pass_grad, i - 8)
        stage(carry_on, i - 4)
        stage(spread_normed, i - 3)
        stage(add_halves, i - 3)
        stage(backward, i - 5)
        stage(give_rows, i - 10)
        stage(far_sum, i - 2)
        stage(row_sums, i - 5)
        stage(add_row_halves, i - 6)
        stage(finish_rows, i - 9)
        return 0

    lax.fori_loop(0, CH + 10, turn, 0)

    def last_arrivals(j, _):
        arrived(HG_SIB, j, hg_sib.at[j])
        arrived(HG_FWD, j, hg_other.at[j])
        arrived(N_SIB, j, n_sib.at[j])
        arrived(N_SHARE, j, n_other.at[j])
        return 0

    lax.fori_loop(0, CH, last_arrivals, 0)
    for load in moments:
        load.wait()

    def product(left_rows, right_rows):
        return lax.dot_general(
            left_rows.reshape(CH * ROWS, TILE), right_rows.reshape(CH * ROWS, 512),
            (((0,), (0,)), ((), ())), preferred_element_type=jnp.float32,
        )

    def step_dir(q, _):
        f = q // 2
        rows = pl.ds(pl.multiple_of(f * TILE, TILE), TILE)
        there = pl.ds(pl.multiple_of(lax.rem(q, 2) * 512, 512), 512)
        total = product(nrm[:, :, :, tile(d, f)], hg[:, :, there])
        total += product(n_sib[:, :, :, rows], hg_sib[:, :, there])
        total += product(n_anti[:, :, :, tile(core, f)], hg_anti[:, :, there])
        total += product(n_other[:, :, :, rows], hg_other[:, :, there])
        total = total * (1.0 / (4 * CH * ROWS))
        pair = pl.ds(lax.rem(f, 2) * 2, 2)
        one = f32(x_all[f // 2, pair, :, :, there]).reshape(TILE, 512)
        two = f32(x_all[2 + f // 2, pair, :, :, there]).reshape(TILE, 512)
        first = BETA_ONE * one + (1.0 - BETA_ONE) * total
        second = BETA_TWO * two + (1.0 - BETA_TWO) * total * total
        value = bf16(first / (jnp.sqrt(second) + 1e-08))
        x_all[f // 2, pair, :, :, there] = value.reshape(2, 4, SLAB, 512)
        return 0

    lax.fori_loop(0, 8, step_dir, 0)
    out = pltpu.make_async_copy(x_all.at[0:2], upd_ref, local_sem.at[14])
    out.start()

    def drain(j, _):
        for k in range(1, 4):
            arrived(Y_ONE + k - 1, j, y_ref.at[j, :, cols(lax.rem(t + 4 - k, 4))])
            sent(Y_ONE + k - 1, j, y_cols.at[j, 0])
        pltpu.make_async_copy(y_cols.at[j, t], y_ref.at[j, :, cols(t)], local_sem.at[6 + j]).wait()
        pltpu.make_async_copy(row_l.at[j], dx_ref.at[j], local_sem.at[10 + j]).wait()
        sent(W_ANTI, j, w_all.at[cols(d), quarter(j)])
        sent(W_FWD, j, w_all.at[cols(anti), quarter(j)])
        for q in range(3):
            sent(X_ONE + q, j, x_all.at[j, :, t])
        sent(GATHER_R, j, in_all.at[j, :, cols(t)])
        sent(GATHER_L, j, in_all.at[j, :, cols(t)])
        sent(RELAY_R, j, in_all.at[j, pl.ds(0, 64), cols(left)])
        sent(RELAY_L, j, in_all.at[j, pl.ds(64, 64), cols(right)])
        sent(OPP_R, j, opp.at[j, pl.ds(0, 64)])
        sent(OPP_L, j, opp.at[j, pl.ds(64, 64)])
        sent(SUM_R, j, to_r.at[j])
        sent(SUM_L, j, to_l.at[j])
        sent(CARRY_MOVE, j, own.at[j])
        sent(ROW_OPP_R, j, part.at[j, across, pl.ds(0, 16)])
        sent(ROW_OPP_L, j, part.at[j, across, pl.ds(16, 16)])
        sent(ROW_SUM_R, j, part.at[j, right])
        sent(ROW_SUM_L, j, part.at[j, left])
        sent(HG_SIB, j, hg.at[j])
        sent(HG_ANTI, j, hg.at[j])
        sent(HG_FWD, j, hg_anti.at[j])
        sent(N_ANTI, j, n_anti.at[j, t])
        sent(N_SIB, j, n_sib.at[j])
        sent(N_R, j, n_anti.at[j, t])
        sent(N_L, j, n_anti.at[j, t])
        sent(N_RELAY_R, j, n_anti.at[j, left, pl.ds(0, 16)])
        sent(N_RELAY_L, j, n_anti.at[j, right, pl.ds(16, 16)])
        sent(N_SHARE, j, n_other.at[j])
        return 0

    lax.fori_loop(0, CH, drain, 0)
    sent(W_SIB, 0, w_all.at[cols(d)])
    for k in range(3):
        sent(C_COLS, k, cot.at[:, t])
    out.wait()


def whole(x, cot, w, m1, m2, gain, flags):
    def vm(*shape, dtype=jnp.bfloat16):
        return pltpu.VMEM(shape, dtype)

    scratch = [
        vm(D, COLS), vm(COLS, D), vm(4, CH, 4, SLAB, COLS), vm(CH, ROWS, D), vm(CH, 4, SLAB, D),
        vm(CH, ROWS, COLS, dtype=jnp.float32), vm(CH, 4, SLAB, COLS),
        vm(CH, 4, SLAB, COLS), vm(CH, ROWS, COLS), vm(CH, 4, SLAB, COLS),
        vm(CH, ROWS, COLS), vm(CH, ROWS, COLS), vm(CH, ROWS, COLS), vm(CH, ROWS, COLS),
        vm(CH, 64, COLS), vm(CH, 64, COLS), vm(CH, ROWS, COLS), vm(CH, ROWS, COLS),
        vm(CH, 4, SLAB, D), vm(CH, 16, D), vm(CH, 16, D), vm(CH, SLAB, D), vm(CH, SLAB, D),
        vm(CH, ROWS, COLS), vm(CH, ROWS, COLS), vm(CH, ROWS, COLS), vm(CH, ROWS, COLS),
        vm(CH, 4, SLAB, COLS), vm(CH, 4, SLAB, 2 * COLS), vm(CH, 4, SLAB, COLS),
        vm(CH, ROWS, 1, dtype=jnp.float32), vm(CH, ROWS, 1, dtype=jnp.float32),
        pltpu.SemaphoreType.DMA((34, CH)), pltpu.SemaphoreType.DMA((34, CH)), pltpu.SemaphoreType.DMA((15,)),
    ]
    anywhere = pl.BlockSpec(memory_space=pl.ANY)
    near = pl.BlockSpec(memory_space=pltpu.VMEM)
    return pl.pallas_call(
        kernel,
        out_shape=(
            jax.ShapeDtypeStruct((CH, SLAB, D), jnp.bfloat16),
            jax.ShapeDtypeStruct((CH, SLAB, D), jnp.bfloat16),
            jax.ShapeDtypeStruct((2, 4, 4, SLAB, COLS), jnp.bfloat16),
        ),
        in_specs=[anywhere] * 5 + [near, pl.BlockSpec(memory_space=pltpu.SMEM)],
        out_specs=(anywhere,) * 3,
        scratch_shapes=scratch,
        compiler_params=pltpu.CompilerParams(
            collective_id=0, has_side_effects=True, vmem_limit_bytes=63 * 2**20
        ),
        cost_estimate=pl.CostEstimate(flops=21 * 10**9, bytes_accessed=20 * 2**20, transcendentals=2 * 10**6),
    )(x, cot, w, m1, m2, gain, flags)


def body(x_in, gain, weight, moment_one, moment_two, cotangent, preempted):
    y, dx, update = whole(
        x_in.reshape(CH, SLAB, D), cotangent.reshape(CH, SLAB, D), weight[0],
        moment_one.reshape(2, 4, 4, SLAB, COLS), moment_two.reshape(2, 4, 4, SLAB, COLS), gain, preempted,
    )
    return (y.reshape(1, CH * SLAB, D), dx.reshape(1, CH * SLAB, D), update.reshape(1, COLS, COLS))


def solution(mesh):
    placed = (
        P("section", ("dp", "tensor"), None),
        P("section", None),
        P("section", "dp", "tensor"),
        P("section", "dp", "tensor"),
        P("section", "dp", "tensor"),
        P("section", ("dp", "tensor"), None),
        P(),
    )
    return jax.shard_map(
        body,
        mesh=mesh,
        in_specs=placed,
        out_specs=(
            P("section", ("dp", "tensor"), None),
            P("section", ("dp", "tensor"), None),
            P("section", "dp", "tensor"),
        ),
        check_vma=False,
    )
```

```python
import jax
import jax.numpy as jnp
from jax import lax
from jax.experimental import pallas as pl
from jax.experimental.pallas import tpu as pltpu
from jax.sharding import PartitionSpec as P

EPSILON = 1e-05
BETA_ONE = 0.9
BETA_TWO = 0.95
GELU_SCALE = 0.7978845608028654
GELU_CUBE = 0.044715

D = 4096
CH = 4
ROWS = 128
SLAB = 32
COLS = 1024
TILE = 256
MESH = pl.DeviceIdType.MESH

(W_ANTI, W_FWD, W_SIB, X_ONE, X_TWO, X_THREE, C_COLS, PRIOR_MOVE, GATHER_R, GATHER_L, RELAY_R, RELAY_L,
 Y_ONE, Y_TWO, Y_THREE,
 OPP_R, OPP_L, SUM_R, SUM_L, CARRY_MOVE, ROW_OPP_R, ROW_OPP_L, ROW_SUM_R, ROW_SUM_L, HG_SIB, HG_ANTI, HG_FWD,
 N_ANTI, N_SIB, N_R, N_L, N_RELAY_R, N_RELAY_L, N_SHARE) = range(34)


def gelu(v):
    return 0.5 * v * (1.0 + jnp.tanh(GELU_SCALE * (v + GELU_CUBE * v * v * v)))


def gelu_slope(v):
    square = v * v
    th = jnp.tanh(GELU_SCALE * v * (1.0 + GELU_CUBE * square))
    return 0.5 * (1.0 + th) + (0.5 * GELU_SCALE) * v * (1.0 - th * th) * (1.0 + 3.0 * GELU_CUBE * square)


def f32(v):
    return v.astype(jnp.float32)


def bf16(v):
    return v.astype(jnp.bfloat16)


def kernel(
    x_ref, cot_ref, w_ref, m1_ref, m2_ref, gain_ref, flag_ref,
    y_ref, dx_ref, upd_ref,
    w_all, w_t, x_all, in_all, nrm, hid, cot, prior, incoming, y_cols,
    opp, to_r, to_l, own, got_a, got_b, got_l, got_r,
    part, row_a, row_b, row_l, row_r,
    hg, hg_sib, hg_anti, hg_other, n_sib, n_anti, n_other, inv_s, total_s,
    send_sem, recv_sem, local_sem,
):
    t = lax.axis_index("tensor")
    d = lax.axis_index("dp")
    s = lax.axis_index("section")
    right, left, across = lax.rem(t + 1, 4), lax.rem(t + 3, 4), lax.rem(t + 2, 4)
    core = lax.rem(d, 2)
    half = d // 2
    sib = d + 1 - 2 * core
    anti = lax.rem(d + 2, 4)
    anti_sib = lax.rem(sib + 2, 4)
    after = lax.rem(s + 1, 16)
    before = lax.rem(s + 15, 16)
    to_right, to_left = {"tensor": right}, {"tensor": left}
    to_sib, to_anti = {"dp": sib}, {"dp": anti}
    to_after, to_before = {"section": after}, {"section": before}

    def cols(block):
        return pl.ds(pl.multiple_of(block * COLS, COLS), COLS)

    def tile(block, n):
        return pl.ds(pl.multiple_of(block * COLS + n * TILE, TILE), TILE)

    def copy(kind, index, src, dst, device):
        return pltpu.make_async_remote_copy(
            src_ref=src, dst_ref=dst, send_sem=send_sem.at[kind, index], recv_sem=recv_sem.at[kind, index],
            device_id=device, device_id_type=MESH,
        )

    def arrived(kind, index, where):
        copy(kind, index, where, where, to_sib).wait_recv()

    def sent(kind, index, where):
        copy(kind, index, where, where, to_sib).wait_send()

    barrier = pltpu.get_barrier_semaphore()
    for device in (to_right, to_left, {"tensor": across}, to_sib, to_anti, to_after, to_before):
        pl.semaphore_signal(barrier, inc=1, device_id=device, device_id_type=MESH)
    pl.semaphore_wait(barrier, 7)

    flag_self = flag_ref[d, s]
    flag_next = flag_ref[d, after]

    def quarter(k):
        return pl.ds(pl.multiple_of(k * TILE, TILE), TILE)

    for k in range(4):
        copy(W_ANTI, k, w_ref.at[:, quarter(k)], w_all.at[cols(d), quarter(k)], to_anti).start()
    copy(W_SIB, 0, w_ref, w_all.at[cols(d)], to_sib).start()
    for b in range(4):
        for k in range(1, 4):
            copy(
                X_ONE + k - 1, b, x_ref.at[:, :, cols(b)], x_all.at[b, :, t], {"tensor": lax.rem(t + k, 4)}
            ).start()
    loads = [pltpu.make_async_copy(x_ref.at[:, :, cols(b)], x_all.at[b, :, t], local_sem.at[b]) for b in range(4)]
    loads += [
        pltpu.make_async_copy(w_ref, w_all.at[cols(d)], local_sem.at[4]),
        pltpu.make_async_copy(cot_ref.at[:, :, cols(t)], cot.at[:, t], local_sem.at[5]),
    ]
    for load in loads:
        load.start()
    for k in range(1, 4):
        peer = lax.rem(t + k, 4)
        copy(C_COLS, k - 1, cot_ref.at[:, :, cols(peer)], cot.at[:, t], {"tensor": peer}).start()

    def normalize(read, j):
        def squares(b, total):
            u = read(b)
            u = u * u
            return total + (u[:, 0:128] + u[:, 128:256]) + (u[:, 256:384] + u[:, 384:512])

        total = lax.fori_loop(0, 8, squares, jnp.zeros((ROWS, 128), jnp.float32))
        inv = lax.rsqrt(jnp.sum(total, axis=-1, keepdims=True) * (1.0 / D) + EPSILON)

        def scale(b, _):
            where = pl.ds(pl.multiple_of(b * 512, 512), 512)
            nrm[j, :, :, where] = bf16(read(b) * inv * f32(gain_ref[:, where])).reshape(4, SLAB, 512)
            return 0

        lax.fori_loop(0, 8, scale, 0)
        return inv

    for b in range(4):
        loads[b].wait()
        for k in range(1, 4):
            arrived(X_ONE + k - 1, b, x_all.at[b, :, lax.rem(t + 4 - k, 4)])

    def first_norm(j, _):
        def read(b):
            where = pl.ds(pl.multiple_of(lax.rem(b, 2) * 512, 512), 512)
            return f32(x_all[b // 2, j, :, :, where]).reshape(ROWS, 512)

        normalize(read, j)
        return 0

    lax.fori_loop(0, CH, first_norm, 0)
    loads[4].wait()
    arrived(W_SIB, 0, w_all.at[cols(sib)])

    def add_rows(block, k, clear=False):
        there = quarter(k)
        product = jnp.dot(
            nrm[:, :, :, cols(block)].reshape(CH * ROWS, COLS), w_all[cols(block), there],
            preferred_element_type=jnp.float32,
        ).reshape(CH, ROWS, TILE)
        if clear:
            hid[:, :, there] = product
        else:
            hid[:, :, there] += product

    def turn_weight(k):
        def step(m, _):
            w_t[quarter(k), quarter(m)] = w_all[quarter(m), quarter(k)].T
            return 0

        lax.fori_loop(0, 16, step, 0)

    def first_tile(j, k):
        there = quarter(k)
        branch = f32(bf16(gelu(hid[j, :, there])))
        value = bf16(f32(x_all[t, j, :, :, there]).reshape(ROWS, TILE) + branch)
        y_cols[j, :, :, there] = value.reshape(4, SLAB, TILE)

    def take(k, _):
        add_rows(d, k, clear=True)
        add_rows(sib, k)
        theirs = w_all.at[cols(anti), quarter(k)]
        arrived(W_ANTI, k, theirs)
        copy(W_FWD, k, theirs, theirs, to_sib).start()
        add_rows(anti, k)
        arrived(W_FWD, k, w_all.at[cols(anti_sib), quarter(k)])
        add_rows(anti_sib, k)

        lax.fori_loop(0, CH, lambda j, _: (first_tile(j, k), 0)[1], 0)
        turn_weight(k)
        return 0

    def take_last(k):
        add_rows(d, k, clear=True)
        add_rows(sib, k)
        theirs = w_all.at[cols(anti), quarter(k)]
        arrived(W_ANTI, k, theirs)
        copy(W_FWD, k, theirs, theirs, to_sib).start()
        add_rows(anti, k)
        arrived(W_FWD, k, w_all.at[cols(anti_sib), quarter(k)])
        add_rows(anti_sib, k)

        def step(j, _):
            first_tile(j, k)
            copy(PRIOR_MOVE, j, y_cols.at[j], prior.at[j], to_after).start()
            return 0

        lax.fori_loop(0, CH, step, 0)
        turn_weight(k)

    lax.fori_loop(0, 3, take, 0)
    take_last(3)
    loads[5].wait()
    for k in range(1, 4):
        arrived(C_COLS, k - 1, cot.at[:, lax.rem(t + 4 - k, 4)])

    moments = [
        pltpu.make_async_copy(m1_ref, x_all.at[0:2], local_sem.at[0]),
        pltpu.make_async_copy(m2_ref, x_all.at[2:4], local_sem.at[1]),
    ]

    def choose(j):
        arrived(PRIOR_MOVE, j, prior.at[j])

        def step(n, _):
            there = quarter(n)
            mask = jnp.full((ROWS, TILE), flag_self, jnp.int32) == 1
            plain = f32(x_all[t, j, :, :, there]).reshape(ROWS, TILE)
            in_all[j, :, tile(t, n)] = bf16(jnp.where(mask, f32(prior[j, :, :, there]).reshape(ROWS, TILE), plain))
            return 0

        lax.fori_loop(0, 4, step, 0)
        mine = in_all.at[j, :, cols(t)]
        copy(GATHER_R, j, mine, mine, to_right).start()
        copy(GATHER_L, j, mine, mine, to_left).start()

        @pl.when(j == CH - 1)
        def _():
            for load in moments:
                load.start()

    def relay(j):
        arrived(GATHER_R, j, in_all.at[j, :, cols(left)])
        low = in_all.at[j, pl.ds(0, 64), cols(left)]
        copy(RELAY_R, j, low, low, to_right).start()
        arrived(GATHER_L, j, in_all.at[j, :, cols(right)])
        high = in_all.at[j, pl.ds(64, 64), cols(right)]
        copy(RELAY_L, j, high, high, to_left).start()

    def input_grad_tile(source, block, m, j, inv, slope):
        rows = tile(block, m)
        normed_grad = jnp.dot(source, w_t[:, rows], preferred_element_type=jnp.float32)
        return normed_grad * (inv * f32(gain_ref[:, rows])) - f32(in_all[j, :, rows]) * slope

    def forward(j):
        arrived(RELAY_R, j, in_all.at[j, pl.ds(0, 64), cols(across)])
        arrived(RELAY_L, j, in_all.at[j, pl.ds(64, 64), cols(across)])
        sent(PRIOR_MOVE, j, y_cols.at[j])
        inv = normalize(lambda b: f32(in_all[j, :, pl.ds(pl.multiple_of(b * 512, 512), 512)]), j)
        inv_s[j] = inv

        def step(n, total):
            there = pl.ds(pl.multiple_of(n * TILE, TILE), TILE)
            hidden = jnp.dot(nrm[j].reshape(ROWS, D), w_all[:, there], preferred_element_type=jnp.float32)
            hid[j, :, there] = hidden
            branch = f32(bf16(gelu(hidden)))
            y_cols[j, :, :, there] = bf16(f32(in_all[j, :, tile(t, n)]) + branch).reshape(4, SLAB, TILE)
            upstream = f32(cot[j, :, :, there]).reshape(ROWS, TILE)
            grad = bf16(upstream * gelu_slope(hidden))
            hg[j, :, there] = grad
            return total + jnp.sum(f32(grad) * hidden, axis=-1, keepdims=True)

        total_s[j] = lax.fori_loop(0, 4, step, jnp.zeros((ROWS, 1), jnp.float32))

    def send_normed(j):
        crossing = pl.ds(pl.multiple_of((1 - half) * 2048, 2048), 2048)
        copy(N_ANTI, j, nrm.at[j, t, :, crossing], n_anti.at[j, t], to_anti).start()
        copy(N_SIB, j, nrm.at[j, :, :, cols(sib)], n_sib.at[j], to_sib).start()

    def fill(target, block, j):
        inv = inv_s[j]
        slope = inv * inv * total_s[j] * (1.0 / D)

        def step(m, _):
            value = bf16(input_grad_tile(hg[j], block, m, j, inv, slope))
            target[j, :, quarter(m)] = value
            return 0

        lax.fori_loop(0, 4, step, 0)

    def far_sum(j):
        fill(opp, across, j)
        copy(OPP_R, j, opp.at[j, pl.ds(0, 64)], got_a.at[j], to_right).start()
        copy(OPP_L, j, opp.at[j, pl.ds(64, 64)], got_b.at[j], to_left).start()

    def near_sums(j):
        fill(to_r, right, j)
        fill(to_l, left, j)
        fill(own, t, j)

    def give_rows(j):
        for k in range(1, 4):
            peer = lax.rem(t + k, 4)
            copy(Y_ONE + k - 1, j, y_cols.at[j, peer], y_ref.at[j, :, cols(t)], {"tensor": peer}).start()
        pltpu.make_async_copy(y_cols.at[j, t], y_ref.at[j, :, cols(t)], local_sem.at[6 + j]).start()

    def add_halves(j):
        arrived(OPP_R, j, got_a.at[j])
        to_r[j, 0:64, :] = bf16(f32(to_r[j, 0:64, :]) + f32(got_a[j]))
        copy(SUM_R, j, to_r.at[j], got_l.at[j], to_right).start()
        arrived(OPP_L, j, got_b.at[j])
        to_l[j, 64:128, :] = bf16(f32(to_l[j, 64:128, :]) + f32(got_b[j]))
        copy(SUM_L, j, to_l.at[j], got_r.at[j], to_left).start()

    def carry_on(j):
        arrived(SUM_R, j, got_l.at[j])
        arrived(SUM_L, j, got_r.at[j])

        def step(n, _):
            there = pl.ds(pl.multiple_of(n * TILE, TILE), TILE)
            total = (f32(got_l[j, :, there]) + f32(got_r[j, :, there])) + f32(own[j, :, there])
            own[j, :, there] = bf16(f32(cot[j, :, :, there]).reshape(ROWS, TILE) + total)
            return 0

        lax.fori_loop(0, 4, step, 0)
        copy(CARRY_MOVE, j, own.at[j], incoming.at[j], to_before).start()

    def backward(j):
        arrived(CARRY_MOVE, j, incoming.at[j])

        def step(n, total):
            there = pl.ds(pl.multiple_of(n * TILE, TILE), TILE)
            mask = jnp.full((ROWS, TILE), flag_next, jnp.int32) == 1
            upstream = f32(cot[j, :, :, there]).reshape(ROWS, TILE)
            summed = bf16(upstream + jnp.where(mask, f32(incoming[j, :, there]), 0.0))
            incoming[j, :, there] = summed
            hidden = hid[j, :, there]
            grad = bf16(f32(summed) * gelu_slope(hidden))
            hg[j, :, there] = grad
            return total + jnp.sum(f32(grad) * hidden, axis=-1, keepdims=True)

        total_s[j] = lax.fori_loop(0, 4, step, jnp.zeros((ROWS, 1), jnp.float32))

    def send_grads(j):
        copy(HG_ANTI, j, hg.at[j], hg_anti.at[j], to_anti).start()
        copy(HG_SIB, j, hg.at[j], hg_sib.at[j], to_sib).start()

    def row_sums(j):
        inv = inv_s[j]
        slope = inv * inv * total_s[j] * (1.0 / D)

        def other(q, _):
            block = lax.rem(t + 1 + q // 4, 4)
            m = lax.rem(q, 4)
            value = bf16(input_grad_tile(hg[j], block, m, j, inv, slope))
            part[j, :, :, tile(block, m)] = value.reshape(4, SLAB, TILE)
            return 0

        lax.fori_loop(0, 12, other, 0)

        def mine(m, _):
            there = pl.ds(pl.multiple_of(m * TILE, TILE), TILE)
            value = input_grad_tile(hg[j], t, m, j, inv, slope) + f32(incoming[j, :, there])
            part[j, :, :, tile(t, m)] = bf16(value).reshape(4, SLAB, TILE)
            return 0

        lax.fori_loop(0, 4, mine, 0)
        copy(ROW_OPP_R, j, part.at[j, across, pl.ds(0, 16)], row_a.at[j], to_right).start()
        copy(ROW_OPP_L, j, part.at[j, across, pl.ds(16, 16)], row_b.at[j], to_left).start()

    def add_row_halves(j):
        arrived(ROW_OPP_R, j, row_a.at[j])
        part[j, right, 0:16, :] = bf16(f32(part[j, right, 0:16, :]) + f32(row_a[j]))
        copy(ROW_SUM_R, j, part.at[j, right], row_l.at[j], to_right).start()
        arrived(ROW_OPP_L, j, row_b.at[j])
        part[j, left, 16:32, :] = bf16(f32(part[j, left, 16:32, :]) + f32(row_b[j]))
        copy(ROW_SUM_L, j, part.at[j, left], row_r.at[j], to_left).start()

    def finish_rows(j):
        arrived(ROW_SUM_R, j, row_l.at[j])
        arrived(ROW_SUM_L, j, row_r.at[j])

        def step(b, _):
            there = pl.ds(pl.multiple_of(b * 1024, 1024), 1024)
            total = (f32(row_l[j, :, there]) + f32(row_r[j, :, there])) + f32(part[j, t, :, there])
            mask = jnp.full((SLAB, 1024), flag_self, jnp.int32) == 1
            row_l[j, :, there] = bf16(jnp.where(mask, 0.0, total))
            return 0

        lax.fori_loop(0, 4, step, 0)
        pltpu.make_async_copy(row_l.at[j], dx_ref.at[j], local_sem.at[10 + j]).start()

    def spread_normed(j):
        arrived(N_ANTI, j, n_anti.at[j, t])
        copy(N_R, j, n_anti.at[j, t], n_anti.at[j, t], to_right).start()
        copy(N_L, j, n_anti.at[j, t], n_anti.at[j, t], to_left).start()

    def relay_normed(j):
        arrived(N_R, j, n_anti.at[j, left])
        low = n_anti.at[j, left, pl.ds(0, 16)]
        copy(N_RELAY_R, j, low, low, to_right).start()
        arrived(N_L, j, n_anti.at[j, right])
        high = n_anti.at[j, right, pl.ds(16, 16)]
        copy(N_RELAY_L, j, high, high, to_left).start()

    def share_normed(j):
        arrived(N_RELAY_R, j, n_anti.at[j, across, pl.ds(0, 16)])
        arrived(N_RELAY_L, j, n_anti.at[j, across, pl.ds(16, 16)])
        theirs = pl.ds(pl.multiple_of((1 - core) * COLS, COLS), COLS)
        copy(N_SHARE, j, n_anti.at[j, :, :, theirs], n_other.at[j], to_sib).start()

    def pass_grad(j):
        arrived(HG_ANTI, j, hg_anti.at[j])
        copy(HG_FWD, j, hg_anti.at[j], hg_other.at[j], to_sib).start()

    def stage(run, j):
        pl.when(jnp.logical_and(j >= 0, j < CH))(lambda: run(j))

    def turn(i, _):
        stage(carry_on, i - 6)
        stage(give_rows, i - 7)
        stage(pass_grad, i - 19)
        stage(relay_normed, i - 9)
        stage(choose, i)
        stage(spread_normed, i - 6)
        stage(relay, i - 1)
        stage(backward, i - 7)
        stage(far_sum, i - 3)
        stage(send_grads, i - 7)
        stage(forward, i - 2)
        stage(add_row_halves, i - 10)
        stage(row_sums, i - 7)
        stage(send_normed, i - 2)
        stage(near_sums, i - 3)
        stage(add_halves, i - 4)
        stage(share_normed, i - 18)
        return 0

    lax.fori_loop(0, CH + 19, turn, 0)

    def last_arrivals(j, _):
        arrived(HG_SIB, j, hg_sib.at[j])
        arrived(HG_FWD, j, hg_other.at[j])
        arrived(N_SIB, j, n_sib.at[j])
        arrived(N_SHARE, j, n_other.at[j])
        return 0

    lax.fori_loop(0, CH, last_arrivals, 0)
    for load in moments:
        load.wait()

    def product(left_rows, right_rows):
        return lax.dot_general(
            left_rows.reshape(CH * ROWS, TILE), right_rows.reshape(CH * ROWS, 512),
            (((0,), (0,)), ((), ())), preferred_element_type=jnp.float32,
        )

    def step_dir(q, _):
        f = q // 2
        rows = pl.ds(pl.multiple_of(f * TILE, TILE), TILE)
        there = pl.ds(pl.multiple_of(lax.rem(q, 2) * 512, 512), 512)
        total = product(nrm[:, :, :, tile(d, f)], hg[:, :, there])
        total += product(n_sib[:, :, :, rows], hg_sib[:, :, there])
        total += product(n_anti[:, :, :, tile(core, f)], hg_anti[:, :, there])
        total += product(n_other[:, :, :, rows], hg_other[:, :, there])
        total = total * (1.0 / (4 * CH * ROWS))
        pair = pl.ds(lax.rem(f, 2) * 2, 2)
        one = f32(x_all[f // 2, pair, :, :, there]).reshape(TILE, 512)
        two = f32(x_all[2 + f // 2, pair, :, :, there]).reshape(TILE, 512)
        first = BETA_ONE * one + (1.0 - BETA_ONE) * total
        second = BETA_TWO * two + (1.0 - BETA_TWO) * total * total
        value = bf16(first / (jnp.sqrt(second) + 1e-08))
        x_all[f // 2, pair, :, :, there] = value.reshape(2, 4, SLAB, 512)
        return 0

    lax.fori_loop(0, 8, step_dir, 0)
    out = pltpu.make_async_copy(x_all.at[0:2], upd_ref, local_sem.at[14])
    out.start()
    lax.fori_loop(0, CH, lambda j, _: (finish_rows(j), 0)[1], 0)

    def drain(j, _):
        for k in range(1, 4):
            arrived(Y_ONE + k - 1, j, y_ref.at[j, :, cols(lax.rem(t + 4 - k, 4))])
            sent(Y_ONE + k - 1, j, y_cols.at[j, 0])
        pltpu.make_async_copy(y_cols.at[j, t], y_ref.at[j, :, cols(t)], local_sem.at[6 + j]).wait()
        pltpu.make_async_copy(row_l.at[j], dx_ref.at[j], local_sem.at[10 + j]).wait()
        sent(W_ANTI, j, w_all.at[cols(d), quarter(j)])
        sent(W_FWD, j, w_all.at[cols(anti), quarter(j)])
        for q in range(3):
            sent(X_ONE + q, j, x_all.at[j, :, t])
        sent(GATHER_R, j, in_all.at[j, :, cols(t)])
        sent(GATHER_L, j, in_all.at[j, :, cols(t)])
        sent(RELAY_R, j, in_all.at[j, pl.ds(0, 64), cols(left)])
        sent(RELAY_L, j, in_all.at[j, pl.ds(64, 64), cols(right)])
        sent(OPP_R, j, opp.at[j, pl.ds(0, 64)])
        sent(OPP_L, j, opp.at[j, pl.ds(64, 64)])
        sent(SUM_R, j, to_r.at[j])
        sent(SUM_L, j, to_l.at[j])
        sent(CARRY_MOVE, j, own.at[j])
        sent(ROW_OPP_R, j, part.at[j, across, pl.ds(0, 16)])
        sent(ROW_OPP_L, j, part.at[j, across, pl.ds(16, 16)])
        sent(ROW_SUM_R, j, part.at[j, right])
        sent(ROW_SUM_L, j, part.at[j, left])
        sent(HG_SIB, j, hg.at[j])
        sent(HG_ANTI, j, hg.at[j])
        sent(HG_FWD, j, hg_anti.at[j])
        sent(N_ANTI, j, n_anti.at[j, t])
        sent(N_SIB, j, n_sib.at[j])
        sent(N_R, j, n_anti.at[j, t])
        sent(N_L, j, n_anti.at[j, t])
        sent(N_RELAY_R, j, n_anti.at[j, left, pl.ds(0, 16)])
        sent(N_RELAY_L, j, n_anti.at[j, right, pl.ds(16, 16)])
        sent(N_SHARE, j, n_other.at[j])
        return 0

    lax.fori_loop(0, CH, drain, 0)
    sent(W_SIB, 0, w_all.at[cols(d)])
    for k in range(3):
        sent(C_COLS, k, cot.at[:, t])
    out.wait()


def whole(x, cot, w, m1, m2, gain, flags):
    def vm(*shape, dtype=jnp.bfloat16):
        return pltpu.VMEM(shape, dtype)

    scratch = [
        vm(D, COLS), vm(COLS, D), vm(4, CH, 4, SLAB, COLS), vm(CH, ROWS, D), vm(CH, 4, SLAB, D),
        vm(CH, ROWS, COLS, dtype=jnp.float32), vm(CH, 4, SLAB, COLS),
        vm(CH, 4, SLAB, COLS), vm(CH, ROWS, COLS), vm(CH, 4, SLAB, COLS),
        vm(CH, ROWS, COLS), vm(CH, ROWS, COLS), vm(CH, ROWS, COLS), vm(CH, ROWS, COLS),
        vm(CH, 64, COLS), vm(CH, 64, COLS), vm(CH, ROWS, COLS), vm(CH, ROWS, COLS),
        vm(CH, 4, SLAB, D), vm(CH, 16, D), vm(CH, 16, D), vm(CH, SLAB, D), vm(CH, SLAB, D),
        vm(CH, ROWS, COLS), vm(CH, ROWS, COLS), vm(CH, ROWS, COLS), vm(CH, ROWS, COLS),
        vm(CH, 4, SLAB, COLS), vm(CH, 4, SLAB, 2 * COLS), vm(CH, 4, SLAB, COLS),
        vm(CH, ROWS, 1, dtype=jnp.float32), vm(CH, ROWS, 1, dtype=jnp.float32),
        pltpu.SemaphoreType.DMA((34, CH)), pltpu.SemaphoreType.DMA((34, CH)), pltpu.SemaphoreType.DMA((15,)),
    ]
    anywhere = pl.BlockSpec(memory_space=pl.ANY)
    near = pl.BlockSpec(memory_space=pltpu.VMEM)
    return pl.pallas_call(
        kernel,
        out_shape=(
            jax.ShapeDtypeStruct((CH, SLAB, D), jnp.bfloat16),
            jax.ShapeDtypeStruct((CH, SLAB, D), jnp.bfloat16),
            jax.ShapeDtypeStruct((2, 4, 4, SLAB, COLS), jnp.bfloat16),
        ),
        in_specs=[anywhere] * 5 + [near, pl.BlockSpec(memory_space=pltpu.SMEM)],
        out_specs=(anywhere,) * 3,
        scratch_shapes=scratch,
        compiler_params=pltpu.CompilerParams(
            collective_id=0, has_side_effects=True, vmem_limit_bytes=63 * 2**20
        ),
        cost_estimate=pl.CostEstimate(flops=21 * 10**9, bytes_accessed=20 * 2**20, transcendentals=2 * 10**6),
    )(x, cot, w, m1, m2, gain, flags)


def body(x_in, gain, weight, moment_one, moment_two, cotangent, preempted):
    y, dx, update = whole(
        x_in.reshape(CH, SLAB, D), cotangent.reshape(CH, SLAB, D), weight[0],
        moment_one.reshape(2, 4, 4, SLAB, COLS), moment_two.reshape(2, 4, 4, SLAB, COLS), gain, preempted,
    )
    return (y.reshape(1, CH * SLAB, D), dx.reshape(1, CH * SLAB, D), update.reshape(1, COLS, COLS))


def solution(mesh):
    placed = (
        P("section", ("dp", "tensor"), None),
        P("section", None),
        P("section", "dp", "tensor"),
        P("section", "dp", "tensor"),
        P("section", "dp", "tensor"),
        P("section", ("dp", "tensor"), None),
        P(),
    )
    return jax.shard_map(
        body,
        mesh=mesh,
        in_specs=placed,
        out_specs=(
            P("section", ("dp", "tensor"), None),
            P("section", ("dp", "tensor"), None),
            P("section", "dp", "tensor"),
        ),
        check_vma=False,
    )
```

```python
import jax
import jax.numpy as jnp
from jax import lax
from jax.experimental import pallas as pl
from jax.experimental.pallas import tpu as pltpu
from jax.sharding import PartitionSpec as P

EPSILON = 1e-05
BETA_ONE = 0.9
BETA_TWO = 0.95
GELU_SCALE = 0.7978845608028654
GELU_CUBE = 0.044715

D = 4096
CH = 4
ROWS = 128
SLAB = 32
COLS = 1024
TILE = 256
MESH = pl.DeviceIdType.MESH

(W_ANTI, W_FWD, W_SIB, X_ONE, X_TWO, X_THREE, C_COLS, PRIOR_MOVE, PRIOR_HIGH, HIGH_R, LOW_L, GATHER_R, GATHER_L, RELAY_R, RELAY_L,
 Y_ONE, Y_TWO, Y_THREE,
 OPP_R, OPP_L, SUM_R, SUM_L, CARRY_MOVE, ROW_OPP_R, ROW_OPP_L, ROW_SUM_R, ROW_SUM_L, HG_SIB, HG_ANTI, HG_FWD,
 N_ANTI, N_SIB, N_R, N_L, N_RELAY_R, N_RELAY_L, N_SHARE) = range(37)


def gelu(v):
    return 0.5 * v * (1.0 + jnp.tanh(GELU_SCALE * (v + GELU_CUBE * v * v * v)))


def gelu_slope(v):
    square = v * v
    th = jnp.tanh(GELU_SCALE * v * (1.0 + GELU_CUBE * square))
    return 0.5 * (1.0 + th) + (0.5 * GELU_SCALE) * v * (1.0 - th * th) * (1.0 + 3.0 * GELU_CUBE * square)


def f32(v):
    return v.astype(jnp.float32)


def bf16(v):
    return v.astype(jnp.bfloat16)


def kernel(
    x_ref, cot_ref, w_ref, m1_ref, m2_ref, gain_ref, flag_ref,
    y_ref, dx_ref, upd_ref,
    w_all, w_t, x_all, in_all, nrm, hid, cot, prior, incoming, y_cols,
    opp, to_r, to_l, own, got_a, got_b, got_l, got_r,
    part, row_a, row_b, row_l, row_r,
    hg, hg_sib, hg_anti, hg_other, n_sib, n_anti, n_other, inv_s, total_s,
    send_sem, recv_sem, local_sem,
):
    t = lax.axis_index("tensor")
    d = lax.axis_index("dp")
    s = lax.axis_index("section")
    right, left, across = lax.rem(t + 1, 4), lax.rem(t + 3, 4), lax.rem(t + 2, 4)
    core = lax.rem(d, 2)
    half = d // 2
    sib = d + 1 - 2 * core
    anti = lax.rem(d + 2, 4)
    anti_sib = lax.rem(sib + 2, 4)
    after = lax.rem(s + 1, 16)
    before = lax.rem(s + 15, 16)
    to_right, to_left = {"tensor": right}, {"tensor": left}
    to_sib, to_anti = {"dp": sib}, {"dp": anti}
    to_after, to_before = {"section": after}, {"section": before}

    def cols(block):
        return pl.ds(pl.multiple_of(block * COLS, COLS), COLS)

    def tile(block, n):
        return pl.ds(pl.multiple_of(block * COLS + n * TILE, TILE), TILE)

    def copy(kind, index, src, dst, device):
        return pltpu.make_async_remote_copy(
            src_ref=src, dst_ref=dst, send_sem=send_sem.at[kind, index], recv_sem=recv_sem.at[kind, index],
            device_id=device, device_id_type=MESH,
        )

    def arrived(kind, index, where):
        copy(kind, index, where, where, to_sib).wait_recv()

    def sent(kind, index, where):
        copy(kind, index, where, where, to_sib).wait_send()

    barrier = pltpu.get_barrier_semaphore()
    for device in (to_right, to_left, {"tensor": across}, to_sib, to_anti, to_after, to_before):
        pl.semaphore_signal(barrier, inc=1, device_id=device, device_id_type=MESH)
    pl.semaphore_wait(barrier, 7)

    flag_self = flag_ref[d, s]
    flag_next = flag_ref[d, after]

    def quarter(k):
        return pl.ds(pl.multiple_of(k * TILE, TILE), TILE)

    for k in range(4):
        copy(W_ANTI, k, w_ref.at[:, quarter(k)], w_all.at[cols(d), quarter(k)], to_anti).start()
    copy(W_SIB, 0, w_ref, w_all.at[cols(d)], to_sib).start()
    for b in range(4):
        for k in range(1, 4):
            copy(
                X_ONE + k - 1, b, x_ref.at[:, :, cols(b)], x_all.at[b, :, t], {"tensor": lax.rem(t + k, 4)}
            ).start()
    loads = [pltpu.make_async_copy(x_ref.at[:, :, cols(b)], x_all.at[b, :, t], local_sem.at[b]) for b in range(4)]
    loads += [
        pltpu.make_async_copy(w_ref, w_all.at[cols(d)], local_sem.at[4]),
        pltpu.make_async_copy(cot_ref.at[:, :, cols(t)], cot.at[:, t], local_sem.at[5]),
    ]
    for load in loads:
        load.start()
    for k in range(1, 4):
        peer = lax.rem(t + k, 4)
        copy(C_COLS, k - 1, cot_ref.at[:, :, cols(peer)], cot.at[:, t], {"tensor": peer}).start()

    def normalize(read, j):
        def squares(b, total):
            u = read(b)
            u = u * u
            return total + (u[:, 0:128] + u[:, 128:256]) + (u[:, 256:384] + u[:, 384:512])

        total = lax.fori_loop(0, 8, squares, jnp.zeros((ROWS, 128), jnp.float32))
        inv = lax.rsqrt(jnp.sum(total, axis=-1, keepdims=True) * (1.0 / D) + EPSILON)

        def scale(b, _):
            where = pl.ds(pl.multiple_of(b * 512, 512), 512)
            nrm[j, :, :, where] = bf16(read(b) * inv * f32(gain_ref[:, where])).reshape(4, SLAB, 512)
            return 0

        lax.fori_loop(0, 8, scale, 0)
        return inv

    for b in range(4):
        loads[b].wait()
        for k in range(1, 4):
            arrived(X_ONE + k - 1, b, x_all.at[b, :, lax.rem(t + 4 - k, 4)])

    def first_norm(j, _):
        def read(b):
            where = pl.ds(pl.multiple_of(lax.rem(b, 2) * 512, 512), 512)
            return f32(x_all[b // 2, j, :, :, where]).reshape(ROWS, 512)

        normalize(read, j)
        return 0

    lax.fori_loop(0, CH, first_norm, 0)
    loads[4].wait()
    arrived(W_SIB, 0, w_all.at[cols(sib)])

    def add_rows(block, k, clear=False):
        there = quarter(k)
        product = jnp.dot(
            nrm[:, :, :, cols(block)].reshape(CH * ROWS, COLS), w_all[cols(block), there],
            preferred_element_type=jnp.float32,
        ).reshape(CH, ROWS, TILE)
        if clear:
            hid[:, :, there] = product
        else:
            hid[:, :, there] += product

    def turn_weight(k):
        def step(m, _):
            w_t[quarter(k), quarter(m)] = w_all[quarter(m), quarter(k)].T
            return 0

        lax.fori_loop(0, 16, step, 0)

    def first_tile(j, k):
        there = quarter(k)
        branch = f32(bf16(gelu(hid[j, :, there])))
        value = bf16(f32(x_all[t, j, :, :, there]).reshape(ROWS, TILE) + branch)
        y_cols[j, :, :, there] = value.reshape(4, SLAB, TILE)

    def take(k, _):
        add_rows(d, k, clear=True)
        add_rows(sib, k)
        theirs = w_all.at[cols(anti), quarter(k)]
        arrived(W_ANTI, k, theirs)
        copy(W_FWD, k, theirs, theirs, to_sib).start()
        add_rows(anti, k)
        arrived(W_FWD, k, w_all.at[cols(anti_sib), quarter(k)])
        add_rows(anti_sib, k)

        lax.fori_loop(0, CH, lambda j, _: (first_tile(j, k), 0)[1], 0)
        turn_weight(k)
        return 0

    def take_last(k):
        add_rows(d, k, clear=True)
        add_rows(sib, k)
        theirs = w_all.at[cols(anti), quarter(k)]
        arrived(W_ANTI, k, theirs)
        copy(W_FWD, k, theirs, theirs, to_sib).start()
        add_rows(anti, k)
        arrived(W_FWD, k, w_all.at[cols(anti_sib), quarter(k)])
        add_rows(anti_sib, k)

        def step(j, _):
            first_tile(j, k)
            for kind, part_of in ((PRIOR_MOVE, pl.ds(0, 2)), (PRIOR_HIGH, pl.ds(2, 2))):
                copy(kind, j, y_cols.at[j, part_of], prior.at[j, part_of], to_after).start()
            return 0

        lax.fori_loop(0, CH, step, 0)
        turn_weight(k)

    lax.fori_loop(0, 3, take, 0)
    take_last(3)
    loads[5].wait()
    for k in range(1, 4):
        arrived(C_COLS, k - 1, cot.at[:, lax.rem(t + 4 - k, 4)])

    moments = [
        pltpu.make_async_copy(m1_ref, x_all.at[0:2], local_sem.at[0]),
        pltpu.make_async_copy(m2_ref, x_all.at[2:4], local_sem.at[1]),
    ]

    def choose_half(j, h):
        slabs, rows = pl.ds(2 * h, 2), pl.ds(64 * h, 64)

        def step(n, _):
            there = quarter(n)
            mask = jnp.full((64, TILE), flag_self, jnp.int32) == 1
            plain = f32(x_all[t, j, slabs, :, there]).reshape(64, TILE)
            value = bf16(jnp.where(mask, f32(prior[j, slabs, :, there]).reshape(64, TILE), plain))
            in_all[j, rows, tile(t, n)] = value
            return 0

        lax.fori_loop(0, 4, step, 0)
        mine = in_all.at[j, rows, cols(t)]
        copy(HIGH_R if h else GATHER_R, j, mine, mine, to_right).start()
        copy(GATHER_L if h else LOW_L, j, mine, mine, to_left).start()

    def choose(j):
        arrived(PRIOR_MOVE, j, prior.at[j, pl.ds(0, 2)])
        choose_half(j, 0)
        arrived(PRIOR_HIGH, j, prior.at[j, pl.ds(2, 2)])
        choose_half(j, 1)

        @pl.when(j == CH - 1)
        def _():
            for load in moments:
                load.start()

    def relay(j):
        arrived(GATHER_R, j, in_all.at[j, pl.ds(0, 64), cols(left)])
        low = in_all.at[j, pl.ds(0, 64), cols(left)]
        copy(RELAY_R, j, low, low, to_right).start()
        arrived(GATHER_L, j, in_all.at[j, pl.ds(64, 64), cols(right)])
        high = in_all.at[j, pl.ds(64, 64), cols(right)]
        copy(RELAY_L, j, high, high, to_left).start()

    def input_grad_tile(source, block, m, j, inv, slope):
        rows = tile(block, m)
        normed_grad = jnp.dot(source, w_t[:, rows], preferred_element_type=jnp.float32)
        return normed_grad * (inv * f32(gain_ref[:, rows])) - f32(in_all[j, :, rows]) * slope

    def forward(j):
        arrived(RELAY_R, j, in_all.at[j, pl.ds(0, 64), cols(across)])
        arrived(RELAY_L, j, in_all.at[j, pl.ds(64, 64), cols(across)])
        arrived(HIGH_R, j, in_all.at[j, pl.ds(64, 64), cols(left)])
        arrived(LOW_L, j, in_all.at[j, pl.ds(0, 64), cols(right)])
        sent(PRIOR_MOVE, j, y_cols.at[j, pl.ds(0, 2)])
        sent(PRIOR_HIGH, j, y_cols.at[j, pl.ds(2, 2)])
        inv = normalize(lambda b: f32(in_all[j, :, pl.ds(pl.multiple_of(b * 512, 512), 512)]), j)
        inv_s[j] = inv

        def step(n, total):
            there = pl.ds(pl.multiple_of(n * TILE, TILE), TILE)
            hidden = jnp.dot(nrm[j].reshape(ROWS, D), w_all[:, there], preferred_element_type=jnp.float32)
            hid[j, :, there] = hidden
            branch = f32(bf16(gelu(hidden)))
            y_cols[j, :, :, there] = bf16(f32(in_all[j, :, tile(t, n)]) + branch).reshape(4, SLAB, TILE)
            upstream = f32(cot[j, :, :, there]).reshape(ROWS, TILE)
            grad = bf16(upstream * gelu_slope(hidden))
            hg[j, :, there] = grad
            return total + jnp.sum(f32(grad) * hidden, axis=-1, keepdims=True)

        total_s[j] = lax.fori_loop(0, 4, step, jnp.zeros((ROWS, 1), jnp.float32))

    def send_normed(j):
        crossing = pl.ds(pl.multiple_of((1 - half) * 2048, 2048), 2048)
        copy(N_ANTI, j, nrm.at[j, t, :, crossing], n_anti.at[j, t], to_anti).start()
        copy(N_SIB, j, nrm.at[j, :, :, cols(sib)], n_sib.at[j], to_sib).start()

    def fill(target, block, j):
        inv = inv_s[j]
        slope = inv * inv * total_s[j] * (1.0 / D)

        def step(m, _):
            value = bf16(input_grad_tile(hg[j], block, m, j, inv, slope))
            target[j, :, quarter(m)] = value
            return 0

        lax.fori_loop(0, 4, step, 0)

    def far_sum(j):
        fill(opp, across, j)
        copy(OPP_R, j, opp.at[j, pl.ds(0, 64)], got_a.at[j], to_right).start()
        copy(OPP_L, j, opp.at[j, pl.ds(64, 64)], got_b.at[j], to_left).start()

    def near_sums(j):
        fill(to_r, right, j)
        fill(to_l, left, j)
        fill(own, t, j)

    def give_rows(j):
        for k in range(1, 4):
            peer = lax.rem(t + k, 4)
            copy(Y_ONE + k - 1, j, y_cols.at[j, peer], y_ref.at[j, :, cols(t)], {"tensor": peer}).start()
        pltpu.make_async_copy(y_cols.at[j, t], y_ref.at[j, :, cols(t)], local_sem.at[6 + j]).start()

    def add_halves(j):
        arrived(OPP_R, j, got_a.at[j])
        to_r[j, 0:64, :] = bf16(f32(to_r[j, 0:64, :]) + f32(got_a[j]))
        copy(SUM_R, j, to_r.at[j], got_l.at[j], to_right).start()
        arrived(OPP_L, j, got_b.at[j])
        to_l[j, 64:128, :] = bf16(f32(to_l[j, 64:128, :]) + f32(got_b[j]))
        copy(SUM_L, j, to_l.at[j], got_r.at[j], to_left).start()

    def carry_on(j):
        arrived(SUM_R, j, got_l.at[j])
        arrived(SUM_L, j, got_r.at[j])

        def step(n, _):
            there = pl.ds(pl.multiple_of(n * TILE, TILE), TILE)
            total = (f32(got_l[j, :, there]) + f32(got_r[j, :, there])) + f32(own[j, :, there])
            own[j, :, there] = bf16(f32(cot[j, :, :, there]).reshape(ROWS, TILE) + total)
            return 0

        lax.fori_loop(0, 4, step, 0)
        copy(CARRY_MOVE, j, own.at[j], incoming.at[j], to_before).start()

    def backward(j):
        arrived(CARRY_MOVE, j, incoming.at[j])

        def step(n, total):
            there = pl.ds(pl.multiple_of(n * TILE, TILE), TILE)
            mask = jnp.full((ROWS, TILE), flag_next, jnp.int32) == 1
            upstream = f32(cot[j, :, :, there]).reshape(ROWS, TILE)
            summed = bf16(upstream + jnp.where(mask, f32(incoming[j, :, there]), 0.0))
            incoming[j, :, there] = summed
            hidden = hid[j, :, there]
            grad = bf16(f32(summed) * gelu_slope(hidden))
            hg[j, :, there] = grad
            return total + jnp.sum(f32(grad) * hidden, axis=-1, keepdims=True)

        total_s[j] = lax.fori_loop(0, 4, step, jnp.zeros((ROWS, 1), jnp.float32))

    def send_grads(j):
        copy(HG_ANTI, j, hg.at[j], hg_anti.at[j], to_anti).start()
        copy(HG_SIB, j, hg.at[j], hg_sib.at[j], to_sib).start()

    def row_sums(j):
        inv = inv_s[j]
        slope = inv * inv * total_s[j] * (1.0 / D)

        def other(q, _):
            block = lax.rem(t + 1 + q // 4, 4)
            m = lax.rem(q, 4)
            value = bf16(input_grad_tile(hg[j], block, m, j, inv, slope))
            part[j, :, :, tile(block, m)] = value.reshape(4, SLAB, TILE)
            return 0

        lax.fori_loop(0, 12, other, 0)

        def mine(m, _):
            there = pl.ds(pl.multiple_of(m * TILE, TILE), TILE)
            value = input_grad_tile(hg[j], t, m, j, inv, slope) + f32(incoming[j, :, there])
            part[j, :, :, tile(t, m)] = bf16(value).reshape(4, SLAB, TILE)
            return 0

        lax.fori_loop(0, 4, mine, 0)
        copy(ROW_OPP_R, j, part.at[j, across, pl.ds(0, 16)], row_a.at[j], to_right).start()
        copy(ROW_OPP_L, j, part.at[j, across, pl.ds(16, 16)], row_b.at[j], to_left).start()

    def add_row_halves(j):
        arrived(ROW_OPP_R, j, row_a.at[j])
        part[j, right, 0:16, :] = bf16(f32(part[j, right, 0:16, :]) + f32(row_a[j]))
        copy(ROW_SUM_R, j, part.at[j, right], row_l.at[j], to_right).start()
        arrived(ROW_OPP_L, j, row_b.at[j])
        part[j, left, 16:32, :] = bf16(f32(part[j, left, 16:32, :]) + f32(row_b[j]))
        copy(ROW_SUM_L, j, part.at[j, left], row_r.at[j], to_left).start()

    def finish_rows(j):
        arrived(ROW_SUM_R, j, row_l.at[j])
        arrived(ROW_SUM_L, j, row_r.at[j])

        def step(b, _):
            there = pl.ds(pl.multiple_of(b * 1024, 1024), 1024)
            total = (f32(row_l[j, :, there]) + f32(row_r[j, :, there])) + f32(part[j, t, :, there])
            mask = jnp.full((SLAB, 1024), flag_self, jnp.int32) == 1
            row_l[j, :, there] = bf16(jnp.where(mask, 0.0, total))
            return 0

        lax.fori_loop(0, 4, step, 0)
        pltpu.make_async_copy(row_l.at[j], dx_ref.at[j], local_sem.at[10 + j]).start()

    def spread_normed(j):
        arrived(N_ANTI, j, n_anti.at[j, t])
        copy(N_R, j, n_anti.at[j, t], n_anti.at[j, t], to_right).start()
        copy(N_L, j, n_anti.at[j, t], n_anti.at[j, t], to_left).start()

    def relay_normed(j):
        arrived(N_R, j, n_anti.at[j, left])
        low = n_anti.at[j, left, pl.ds(0, 16)]
        copy(N_RELAY_R, j, low, low, to_right).start()
        arrived(N_L, j, n_anti.at[j, right])
        high = n_anti.at[j, right, pl.ds(16, 16)]
        copy(N_RELAY_L, j, high, high, to_left).start()

    def share_normed(j):
        arrived(N_RELAY_R, j, n_anti.at[j, across, pl.ds(0, 16)])
        arrived(N_RELAY_L, j, n_anti.at[j, across, pl.ds(16, 16)])
        theirs = pl.ds(pl.multiple_of((1 - core) * COLS, COLS), COLS)
        copy(N_SHARE, j, n_anti.at[j, :, :, theirs], n_other.at[j], to_sib).start()

    def pass_grad(j):
        arrived(HG_ANTI, j, hg_anti.at[j])
        copy(HG_FWD, j, hg_anti.at[j], hg_other.at[j], to_sib).start()

    def stage(run, j):
        pl.when(jnp.logical_and(j >= 0, j < CH))(lambda: run(j))

    def turn(i, _):
        stage(carry_on, i - 6)
        stage(give_rows, i - 7)
        stage(pass_grad, i - 19)
        stage(relay_normed, i - 9)
        stage(choose, i)
        stage(spread_normed, i - 6)
        stage(relay, i - 1)
        stage(backward, i - 7)
        stage(far_sum, i - 3)
        stage(send_grads, i - 7)
        stage(forward, i - 2)
        stage(add_row_halves, i - 10)
        stage(row_sums, i - 7)
        stage(send_normed, i - 2)
        stage(near_sums, i - 3)
        stage(add_halves, i - 4)
        stage(share_normed, i - 18)
        return 0

    lax.fori_loop(0, CH + 19, turn, 0)

    def last_arrivals(j, _):
        arrived(HG_SIB, j, hg_sib.at[j])
        arrived(HG_FWD, j, hg_other.at[j])
        arrived(N_SIB, j, n_sib.at[j])
        arrived(N_SHARE, j, n_other.at[j])
        return 0

    lax.fori_loop(0, CH, last_arrivals, 0)
    for load in moments:
        load.wait()

    def product(left_rows, right_rows):
        return lax.dot_general(
            left_rows.reshape(CH * ROWS, TILE), right_rows.reshape(CH * ROWS, 512),
            (((0,), (0,)), ((), ())), preferred_element_type=jnp.float32,
        )

    def step_dir(q, _):
        f = q // 2
        rows = pl.ds(pl.multiple_of(f * TILE, TILE), TILE)
        there = pl.ds(pl.multiple_of(lax.rem(q, 2) * 512, 512), 512)
        total = product(nrm[:, :, :, tile(d, f)], hg[:, :, there])
        total += product(n_sib[:, :, :, rows], hg_sib[:, :, there])
        total += product(n_anti[:, :, :, tile(core, f)], hg_anti[:, :, there])
        total += product(n_other[:, :, :, rows], hg_other[:, :, there])
        total = total * (1.0 / (4 * CH * ROWS))
        pair = pl.ds(lax.rem(f, 2) * 2, 2)
        one = f32(x_all[f // 2, pair, :, :, there]).reshape(TILE, 512)
        two = f32(x_all[2 + f // 2, pair, :, :, there]).reshape(TILE, 512)
        first = BETA_ONE * one + (1.0 - BETA_ONE) * total
        second = BETA_TWO * two + (1.0 - BETA_TWO) * total * total
        value = bf16(first / (jnp.sqrt(second) + 1e-08))
        x_all[f // 2, pair, :, :, there] = value.reshape(2, 4, SLAB, 512)
        return 0

    lax.fori_loop(0, 8, step_dir, 0)
    out = pltpu.make_async_copy(x_all.at[0:2], upd_ref, local_sem.at[14])
    out.start()
    lax.fori_loop(0, CH, lambda j, _: (finish_rows(j), 0)[1], 0)

    def drain(j, _):
        for k in range(1, 4):
            arrived(Y_ONE + k - 1, j, y_ref.at[j, :, cols(lax.rem(t + 4 - k, 4))])
            sent(Y_ONE + k - 1, j, y_cols.at[j, 0])
        pltpu.make_async_copy(y_cols.at[j, t], y_ref.at[j, :, cols(t)], local_sem.at[6 + j]).wait()
        pltpu.make_async_copy(row_l.at[j], dx_ref.at[j], local_sem.at[10 + j]).wait()
        sent(W_ANTI, j, w_all.at[cols(d), quarter(j)])
        sent(W_FWD, j, w_all.at[cols(anti), quarter(j)])
        for q in range(3):
            sent(X_ONE + q, j, x_all.at[j, :, t])
        sent(GATHER_R, j, in_all.at[j, pl.ds(0, 64), cols(t)])
        sent(HIGH_R, j, in_all.at[j, pl.ds(64, 64), cols(t)])
        sent(LOW_L, j, in_all.at[j, pl.ds(0, 64), cols(t)])
        sent(GATHER_L, j, in_all.at[j, pl.ds(64, 64), cols(t)])
        sent(RELAY_R, j, in_all.at[j, pl.ds(0, 64), cols(left)])
        sent(RELAY_L, j, in_all.at[j, pl.ds(64, 64), cols(right)])
        sent(OPP_R, j, opp.at[j, pl.ds(0, 64)])
        sent(OPP_L, j, opp.at[j, pl.ds(64, 64)])
        sent(SUM_R, j, to_r.at[j])
        sent(SUM_L, j, to_l.at[j])
        sent(CARRY_MOVE, j, own.at[j])
        sent(ROW_OPP_R, j, part.at[j, across, pl.ds(0, 16)])
        sent(ROW_OPP_L, j, part.at[j, across, pl.ds(16, 16)])
        sent(ROW_SUM_R, j, part.at[j, right])
        sent(ROW_SUM_L, j, part.at[j, left])
        sent(HG_SIB, j, hg.at[j])
        sent(HG_ANTI, j, hg.at[j])
        sent(HG_FWD, j, hg_anti.at[j])
        sent(N_ANTI, j, n_anti.at[j, t])
        sent(N_SIB, j, n_sib.at[j])
        sent(N_R, j, n_anti.at[j, t])
        sent(N_L, j, n_anti.at[j, t])
        sent(N_RELAY_R, j, n_anti.at[j, left, pl.ds(0, 16)])
        sent(N_RELAY_L, j, n_anti.at[j, right, pl.ds(16, 16)])
        sent(N_SHARE, j, n_other.at[j])
        return 0

    lax.fori_loop(0, CH, drain, 0)
    sent(W_SIB, 0, w_all.at[cols(d)])
    for k in range(3):
        sent(C_COLS, k, cot.at[:, t])
    out.wait()


def whole(x, cot, w, m1, m2, gain, flags):
    def vm(*shape, dtype=jnp.bfloat16):
        return pltpu.VMEM(shape, dtype)

    scratch = [
        vm(D, COLS), vm(COLS, D), vm(4, CH, 4, SLAB, COLS), vm(CH, ROWS, D), vm(CH, 4, SLAB, D),
        vm(CH, ROWS, COLS, dtype=jnp.float32), vm(CH, 4, SLAB, COLS),
        vm(CH, 4, SLAB, COLS), vm(CH, ROWS, COLS), vm(CH, 4, SLAB, COLS),
        vm(CH, ROWS, COLS), vm(CH, ROWS, COLS), vm(CH, ROWS, COLS), vm(CH, ROWS, COLS),
        vm(CH, 64, COLS), vm(CH, 64, COLS), vm(CH, ROWS, COLS), vm(CH, ROWS, COLS),
        vm(CH, 4, SLAB, D), vm(CH, 16, D), vm(CH, 16, D), vm(CH, SLAB, D), vm(CH, SLAB, D),
        vm(CH, ROWS, COLS), vm(CH, ROWS, COLS), vm(CH, ROWS, COLS), vm(CH, ROWS, COLS),
        vm(CH, 4, SLAB, COLS), vm(CH, 4, SLAB, 2 * COLS), vm(CH, 4, SLAB, COLS),
        vm(CH, ROWS, 1, dtype=jnp.float32), vm(CH, ROWS, 1, dtype=jnp.float32),
        pltpu.SemaphoreType.DMA((37, CH)), pltpu.SemaphoreType.DMA((37, CH)), pltpu.SemaphoreType.DMA((15,)),
    ]
    anywhere = pl.BlockSpec(memory_space=pl.ANY)
    near = pl.BlockSpec(memory_space=pltpu.VMEM)
    return pl.pallas_call(
        kernel,
        out_shape=(
            jax.ShapeDtypeStruct((CH, SLAB, D), jnp.bfloat16),
            jax.ShapeDtypeStruct((CH, SLAB, D), jnp.bfloat16),
            jax.ShapeDtypeStruct((2, 4, 4, SLAB, COLS), jnp.bfloat16),
        ),
        in_specs=[anywhere] * 5 + [near, pl.BlockSpec(memory_space=pltpu.SMEM)],
        out_specs=(anywhere,) * 3,
        scratch_shapes=scratch,
        compiler_params=pltpu.CompilerParams(
            collective_id=0, has_side_effects=True, vmem_limit_bytes=63 * 2**20
        ),
        cost_estimate=pl.CostEstimate(flops=21 * 10**9, bytes_accessed=20 * 2**20, transcendentals=2 * 10**6),
    )(x, cot, w, m1, m2, gain, flags)


def body(x_in, gain, weight, moment_one, moment_two, cotangent, preempted):
    y, dx, update = whole(
        x_in.reshape(CH, SLAB, D), cotangent.reshape(CH, SLAB, D), weight[0],
        moment_one.reshape(2, 4, 4, SLAB, COLS), moment_two.reshape(2, 4, 4, SLAB, COLS), gain, preempted,
    )
    return (y.reshape(1, CH * SLAB, D), dx.reshape(1, CH * SLAB, D), update.reshape(1, COLS, COLS))


def solution(mesh):
    placed = (
        P("section", ("dp", "tensor"), None),
        P("section", None),
        P("section", "dp", "tensor"),
        P("section", "dp", "tensor"),
        P("section", "dp", "tensor"),
        P("section", ("dp", "tensor"), None),
        P(),
    )
    return jax.shard_map(
        body,
        mesh=mesh,
        in_specs=placed,
        out_specs=(
            P("section", ("dp", "tensor"), None),
            P("section", ("dp", "tensor"), None),
            P("section", "dp", "tensor"),
        ),
        check_vma=False,
    )
```

```python
import jax
import jax.numpy as jnp
from jax import lax
from jax.experimental import pallas as pl
from jax.experimental.pallas import tpu as pltpu
from jax.sharding import PartitionSpec as P

EPSILON = 1e-05
BETA_ONE = 0.9
BETA_TWO = 0.95
GELU_SCALE = 0.7978845608028654
GELU_CUBE = 0.044715

D = 4096
CH = 4
ROWS = 128
SLAB = 32
COLS = 1024
TILE = 256
MESH = pl.DeviceIdType.MESH

(W_ANTI, W_FWD, W_SIB, X_ONE, X_TWO, X_THREE, C_COLS, PRIOR_MOVE, PRIOR_HIGH, HIGH_R, LOW_L, GATHER_R, GATHER_L, RELAY_R, RELAY_L,
 Y_ONE, Y_TWO, Y_THREE,
 OPP_R, OPP_L, SUM_R, SUM_L, CARRY_MOVE, ROW_OPP_R, ROW_OPP_L, ROW_SUM_R, ROW_SUM_L, HG_SIB, HG_ANTI, HG_FWD,
 N_ANTI, N_SIB, N_R, N_L, N_RELAY_R, N_RELAY_L, N_SHARE) = range(37)


def gelu(v):
    return 0.5 * v * (1.0 + jnp.tanh(GELU_SCALE * (v + GELU_CUBE * v * v * v)))


def gelu_slope(v):
    square = v * v
    th = jnp.tanh(GELU_SCALE * v * (1.0 + GELU_CUBE * square))
    return 0.5 * (1.0 + th) + (0.5 * GELU_SCALE) * v * (1.0 - th * th) * (1.0 + 3.0 * GELU_CUBE * square)


def f32(v):
    return v.astype(jnp.float32)


def bf16(v):
    return v.astype(jnp.bfloat16)


def kernel(
    x_ref, cot_ref, w_ref, m1_ref, m2_ref, gain_ref, flag_ref,
    y_ref, dx_ref, upd_ref,
    w_all, w_t, x_all, in_all, nrm, hid, cot, prior, incoming, y_cols,
    opp, to_r, to_l, own, got_a, got_b, got_l, got_r,
    part, row_a, row_b, row_l, row_r,
    hg, hg_sib, hg_anti, hg_other, n_sib, n_anti, n_other, inv_s, total_s,
    send_sem, recv_sem, local_sem,
):
    t = lax.axis_index("tensor")
    d = lax.axis_index("dp")
    s = lax.axis_index("section")
    right, left, across = lax.rem(t + 1, 4), lax.rem(t + 3, 4), lax.rem(t + 2, 4)
    core = lax.rem(d, 2)
    half = d // 2
    sib = d + 1 - 2 * core
    anti = lax.rem(d + 2, 4)
    anti_sib = lax.rem(sib + 2, 4)
    after = lax.rem(s + 1, 16)
    before = lax.rem(s + 15, 16)
    to_right, to_left = {"tensor": right}, {"tensor": left}
    to_sib, to_anti = {"dp": sib}, {"dp": anti}
    to_after, to_before = {"section": after}, {"section": before}

    def cols(block):
        return pl.ds(pl.multiple_of(block * COLS, COLS), COLS)

    def tile(block, n):
        return pl.ds(pl.multiple_of(block * COLS + n * TILE, TILE), TILE)

    def copy(kind, index, src, dst, device):
        return pltpu.make_async_remote_copy(
            src_ref=src, dst_ref=dst, send_sem=send_sem.at[kind, index], recv_sem=recv_sem.at[kind, index],
            device_id=device, device_id_type=MESH,
        )

    def arrived(kind, index, where):
        copy(kind, index, where, where, to_sib).wait_recv()

    def sent(kind, index, where):
        copy(kind, index, where, where, to_sib).wait_send()

    barrier = pltpu.get_barrier_semaphore()
    for device in (to_right, to_left, {"tensor": across}, to_sib, to_anti, to_after, to_before):
        pl.semaphore_signal(barrier, inc=1, device_id=device, device_id_type=MESH)
    pl.semaphore_wait(barrier, 7)

    flag_self = flag_ref[d, s]
    flag_next = flag_ref[d, after]

    def quarter(k):
        return pl.ds(pl.multiple_of(k * TILE, TILE), TILE)

    pieces = ((W_ANTI, W_FWD, 3, 3, pl.ds(768, 128)), (W_SIB, W_SIB, 1, 2, pl.ds(896, 128)))
    for k in range(3):
        copy(W_ANTI, k, w_ref.at[:, quarter(k)], w_all.at[cols(d), quarter(k)], to_anti).start()
    for kind, _, index, _, there in pieces:
        copy(kind, index, w_ref.at[:, there], w_all.at[cols(d), there], to_anti).start()
    copy(W_SIB, 0, w_ref, w_all.at[cols(d)], to_sib).start()
    for b in range(4):
        for k in range(1, 4):
            copy(
                X_ONE + k - 1, b, x_ref.at[:, :, cols(b)], x_all.at[b, :, t], {"tensor": lax.rem(t + k, 4)}
            ).start()
    loads = [pltpu.make_async_copy(x_ref.at[:, :, cols(b)], x_all.at[b, :, t], local_sem.at[b]) for b in range(4)]
    loads += [
        pltpu.make_async_copy(w_ref, w_all.at[cols(d)], local_sem.at[4]),
        pltpu.make_async_copy(cot_ref.at[:, :, cols(t)], cot.at[:, t], local_sem.at[5]),
    ]
    for load in loads:
        load.start()
    for k in range(1, 4):
        peer = lax.rem(t + k, 4)
        copy(C_COLS, k - 1, cot_ref.at[:, :, cols(peer)], cot.at[:, t], {"tensor": peer}).start()

    def normalize(read, j):
        def squares(b, total):
            u = read(b)
            u = u * u
            return total + (u[:, 0:128] + u[:, 128:256]) + (u[:, 256:384] + u[:, 384:512])

        total = lax.fori_loop(0, 8, squares, jnp.zeros((ROWS, 128), jnp.float32))
        inv = lax.rsqrt(jnp.sum(total, axis=-1, keepdims=True) * (1.0 / D) + EPSILON)

        def scale(b, _):
            where = pl.ds(pl.multiple_of(b * 512, 512), 512)
            nrm[j, :, :, where] = bf16(read(b) * inv * f32(gain_ref[:, where])).reshape(4, SLAB, 512)
            return 0

        lax.fori_loop(0, 8, scale, 0)
        return inv

    for b in range(4):
        loads[b].wait()
        for k in range(1, 4):
            arrived(X_ONE + k - 1, b, x_all.at[b, :, lax.rem(t + 4 - k, 4)])

    def first_norm(j, _):
        def read(b):
            where = pl.ds(pl.multiple_of(lax.rem(b, 2) * 512, 512), 512)
            return f32(x_all[b // 2, j, :, :, where]).reshape(ROWS, 512)

        normalize(read, j)
        return 0

    lax.fori_loop(0, CH, first_norm, 0)
    loads[4].wait()
    arrived(W_SIB, 0, w_all.at[cols(sib)])

    def add_rows(block, k, clear=False):
        there = quarter(k)
        product = jnp.dot(
            nrm[:, :, :, cols(block)].reshape(CH * ROWS, COLS), w_all[cols(block), there],
            preferred_element_type=jnp.float32,
        ).reshape(CH, ROWS, TILE)
        if clear:
            hid[:, :, there] = product
        else:
            hid[:, :, there] += product

    def turn_weight(k):
        def step(m, _):
            w_t[quarter(k), quarter(m)] = w_all[quarter(m), quarter(k)].T
            return 0

        lax.fori_loop(0, 16, step, 0)

    def first_tile(j, k):
        there = quarter(k)
        branch = f32(bf16(gelu(hid[j, :, there])))
        value = bf16(f32(x_all[t, j, :, :, there]).reshape(ROWS, TILE) + branch)
        y_cols[j, :, :, there] = value.reshape(4, SLAB, TILE)

    def take(k, _):
        add_rows(d, k, clear=True)
        add_rows(sib, k)
        theirs = w_all.at[cols(anti), quarter(k)]
        arrived(W_ANTI, k, theirs)
        copy(W_FWD, k, theirs, theirs, to_sib).start()
        add_rows(anti, k)
        arrived(W_FWD, k, w_all.at[cols(anti_sib), quarter(k)])
        add_rows(anti_sib, k)

        lax.fori_loop(0, CH, lambda j, _: (first_tile(j, k), 0)[1], 0)
        turn_weight(k)
        return 0

    def take_last(k):
        add_rows(d, k, clear=True)
        add_rows(sib, k)
        for kind, onward, index, at, there in pieces:
            theirs = w_all.at[cols(anti), there]
            arrived(kind, index, theirs)
            copy(onward, at, theirs, theirs, to_sib).start()
        add_rows(anti, k)
        for _, onward, _, at, there in pieces:
            arrived(onward, at, w_all.at[cols(anti_sib), there])
        add_rows(anti_sib, k)

        def step(j, _):
            first_tile(j, k)
            for kind, part_of in ((PRIOR_MOVE, pl.ds(0, 2)), (PRIOR_HIGH, pl.ds(2, 2))):
                copy(kind, j, y_cols.at[j, part_of], prior.at[j, part_of], to_after).start()
            return 0

        lax.fori_loop(0, CH, step, 0)
        turn_weight(k)

    lax.fori_loop(0, 3, take, 0)
    take_last(3)
    loads[5].wait()
    for k in range(1, 4):
        arrived(C_COLS, k - 1, cot.at[:, lax.rem(t + 4 - k, 4)])

    moments = [
        pltpu.make_async_copy(m1_ref, x_all.at[0:2], local_sem.at[0]),
        pltpu.make_async_copy(m2_ref, x_all.at[2:4], local_sem.at[1]),
    ]

    def choose_half(j, h):
        slabs, rows = pl.ds(2 * h, 2), pl.ds(64 * h, 64)

        def step(n, _):
            there = quarter(n)
            mask = jnp.full((64, TILE), flag_self, jnp.int32) == 1
            plain = f32(x_all[t, j, slabs, :, there]).reshape(64, TILE)
            value = bf16(jnp.where(mask, f32(prior[j, slabs, :, there]).reshape(64, TILE), plain))
            in_all[j, rows, tile(t, n)] = value
            return 0

        lax.fori_loop(0, 4, step, 0)
        mine = in_all.at[j, rows, cols(t)]
        copy(HIGH_R if h else GATHER_R, j, mine, mine, to_right).start()
        copy(GATHER_L if h else LOW_L, j, mine, mine, to_left).start()

    def choose(j):
        arrived(PRIOR_MOVE, j, prior.at[j, pl.ds(0, 2)])
        choose_half(j, 0)
        arrived(PRIOR_HIGH, j, prior.at[j, pl.ds(2, 2)])
        choose_half(j, 1)

        @pl.when(j == CH - 1)
        def _():
            for load in moments:
                load.start()

    def relay(j):
        arrived(GATHER_R, j, in_all.at[j, pl.ds(0, 64), cols(left)])
        low = in_all.at[j, pl.ds(0, 64), cols(left)]
        copy(RELAY_R, j, low, low, to_right).start()
        arrived(GATHER_L, j, in_all.at[j, pl.ds(64, 64), cols(right)])
        high = in_all.at[j, pl.ds(64, 64), cols(right)]
        copy(RELAY_L, j, high, high, to_left).start()

    def input_grad_tile(source, block, m, j, inv, slope):
        rows = tile(block, m)
        normed_grad = jnp.dot(source, w_t[:, rows], preferred_element_type=jnp.float32)
        return normed_grad * (inv * f32(gain_ref[:, rows])) - f32(in_all[j, :, rows]) * slope

    def forward(j):
        arrived(RELAY_R, j, in_all.at[j, pl.ds(0, 64), cols(across)])
        arrived(RELAY_L, j, in_all.at[j, pl.ds(64, 64), cols(across)])
        arrived(HIGH_R, j, in_all.at[j, pl.ds(64, 64), cols(left)])
        arrived(LOW_L, j, in_all.at[j, pl.ds(0, 64), cols(right)])
        sent(PRIOR_MOVE, j, y_cols.at[j, pl.ds(0, 2)])
        sent(PRIOR_HIGH, j, y_cols.at[j, pl.ds(2, 2)])
        inv = normalize(lambda b: f32(in_all[j, :, pl.ds(pl.multiple_of(b * 512, 512), 512)]), j)
        inv_s[j] = inv

        def step(n, total):
            there = pl.ds(pl.multiple_of(n * TILE, TILE), TILE)
            hidden = jnp.dot(nrm[j].reshape(ROWS, D), w_all[:, there], preferred_element_type=jnp.float32)
            hid[j, :, there] = hidden
            branch = f32(bf16(gelu(hidden)))
            y_cols[j, :, :, there] = bf16(f32(in_all[j, :, tile(t, n)]) + branch).reshape(4, SLAB, TILE)
            upstream = f32(cot[j, :, :, there]).reshape(ROWS, TILE)
            grad = bf16(upstream * gelu_slope(hidden))
            hg[j, :, there] = grad
            return total + jnp.sum(f32(grad) * hidden, axis=-1, keepdims=True)

        total_s[j] = lax.fori_loop(0, 4, step, jnp.zeros((ROWS, 1), jnp.float32))

    def send_normed(j):
        crossing = pl.ds(pl.multiple_of((1 - half) * 2048, 2048), 2048)
        copy(N_ANTI, j, nrm.at[j, t, :, crossing], n_anti.at[j, t], to_anti).start()
        copy(N_SIB, j, nrm.at[j, :, :, cols(sib)], n_sib.at[j], to_sib).start()

    def fill(target, block, j):
        inv = inv_s[j]
        slope = inv * inv * total_s[j] * (1.0 / D)

        def step(m, _):
            value = bf16(input_grad_tile(hg[j], block, m, j, inv, slope))
            target[j, :, quarter(m)] = value
            return 0

        lax.fori_loop(0, 4, step, 0)

    def far_sum(j):
        fill(opp, across, j)
        copy(OPP_R, j, opp.at[j, pl.ds(0, 64)], got_a.at[j], to_right).start()
        copy(OPP_L, j, opp.at[j, pl.ds(64, 64)], got_b.at[j], to_left).start()

    def near_sums(j):
        fill(to_r, right, j)
        fill(to_l, left, j)
        fill(own, t, j)

    def give_rows(j):
        for k in range(1, 4):
            peer = lax.rem(t + k, 4)
            copy(Y_ONE + k - 1, j, y_cols.at[j, peer], y_ref.at[j, :, cols(t)], {"tensor": peer}).start()
        pltpu.make_async_copy(y_cols.at[j, t], y_ref.at[j, :, cols(t)], local_sem.at[6 + j]).start()

    def add_halves(j):
        arrived(OPP_R, j, got_a.at[j])
        to_r[j, 0:64, :] = bf16(f32(to_r[j, 0:64, :]) + f32(got_a[j]))
        copy(SUM_R, j, to_r.at[j], got_l.at[j], to_right).start()
        arrived(OPP_L, j, got_b.at[j])
        to_l[j, 64:128, :] = bf16(f32(to_l[j, 64:128, :]) + f32(got_b[j]))
        copy(SUM_L, j, to_l.at[j], got_r.at[j], to_left).start()

    def carry_on(j):
        arrived(SUM_R, j, got_l.at[j])
        arrived(SUM_L, j, got_r.at[j])

        def step(n, _):
            there = pl.ds(pl.multiple_of(n * TILE, TILE), TILE)
            total = (f32(got_l[j, :, there]) + f32(got_r[j, :, there])) + f32(own[j, :, there])
            own[j, :, there] = bf16(f32(cot[j, :, :, there]).reshape(ROWS, TILE) + total)
            return 0

        lax.fori_loop(0, 4, step, 0)
        copy(CARRY_MOVE, j, own.at[j], incoming.at[j], to_before).start()

    def backward(j):
        arrived(CARRY_MOVE, j, incoming.at[j])

        def step(n, total):
            there = pl.ds(pl.multiple_of(n * TILE, TILE), TILE)
            mask = jnp.full((ROWS, TILE), flag_next, jnp.int32) == 1
            upstream = f32(cot[j, :, :, there]).reshape(ROWS, TILE)
            summed = bf16(upstream + jnp.where(mask, f32(incoming[j, :, there]), 0.0))
            incoming[j, :, there] = summed
            hidden = hid[j, :, there]
            grad = bf16(f32(summed) * gelu_slope(hidden))
            hg[j, :, there] = grad
            return total + jnp.sum(f32(grad) * hidden, axis=-1, keepdims=True)

        total_s[j] = lax.fori_loop(0, 4, step, jnp.zeros((ROWS, 1), jnp.float32))

    def send_grads(j):
        copy(HG_ANTI, j, hg.at[j], hg_anti.at[j], to_anti).start()
        copy(HG_SIB, j, hg.at[j], hg_sib.at[j], to_sib).start()

    def row_sums(j):
        inv = inv_s[j]
        slope = inv * inv * total_s[j] * (1.0 / D)

        def other(q, _):
            block = lax.rem(t + 1 + q // 4, 4)
            m = lax.rem(q, 4)
            value = bf16(input_grad_tile(hg[j], block, m, j, inv, slope))
            part[j, :, :, tile(block, m)] = value.reshape(4, SLAB, TILE)
            return 0

        lax.fori_loop(0, 12, other, 0)

        def mine(m, _):
            there = pl.ds(pl.multiple_of(m * TILE, TILE), TILE)
            value = input_grad_tile(hg[j], t, m, j, inv, slope) + f32(incoming[j, :, there])
            part[j, :, :, tile(t, m)] = bf16(value).reshape(4, SLAB, TILE)
            return 0

        lax.fori_loop(0, 4, mine, 0)
        copy(ROW_OPP_R, j, part.at[j, across, pl.ds(0, 16)], row_a.at[j], to_right).start()
        copy(ROW_OPP_L, j, part.at[j, across, pl.ds(16, 16)], row_b.at[j], to_left).start()

    def add_row_halves(j):
        arrived(ROW_OPP_R, j, row_a.at[j])
        part[j, right, 0:16, :] = bf16(f32(part[j, right, 0:16, :]) + f32(row_a[j]))
        copy(ROW_SUM_R, j, part.at[j, right], row_l.at[j], to_right).start()
        arrived(ROW_OPP_L, j, row_b.at[j])
        part[j, left, 16:32, :] = bf16(f32(part[j, left, 16:32, :]) + f32(row_b[j]))
        copy(ROW_SUM_L, j, part.at[j, left], row_r.at[j], to_left).start()

    def finish_rows(j):
        arrived(ROW_SUM_R, j, row_l.at[j])
        arrived(ROW_SUM_L, j, row_r.at[j])

        def step(b, _):
            there = pl.ds(pl.multiple_of(b * 1024, 1024), 1024)
            total = (f32(row_l[j, :, there]) + f32(row_r[j, :, there])) + f32(part[j, t, :, there])
            mask = jnp.full((SLAB, 1024), flag_self, jnp.int32) == 1
            row_l[j, :, there] = bf16(jnp.where(mask, 0.0, total))
            return 0

        lax.fori_loop(0, 4, step, 0)
        pltpu.make_async_copy(row_l.at[j], dx_ref.at[j], local_sem.at[10 + j]).start()

    def spread_normed(j):
        arrived(N_ANTI, j, n_anti.at[j, t])
        copy(N_R, j, n_anti.at[j, t], n_anti.at[j, t], to_right).start()
        copy(N_L, j, n_anti.at[j, t], n_anti.at[j, t], to_left).start()

    def relay_normed(j):
        arrived(N_R, j, n_anti.at[j, left])
        low = n_anti.at[j, left, pl.ds(0, 16)]
        copy(N_RELAY_R, j, low, low, to_right).start()
        arrived(N_L, j, n_anti.at[j, right])
        high = n_anti.at[j, right, pl.ds(16, 16)]
        copy(N_RELAY_L, j, high, high, to_left).start()

    def share_normed(j):
        arrived(N_RELAY_R, j, n_anti.at[j, across, pl.ds(0, 16)])
        arrived(N_RELAY_L, j, n_anti.at[j, across, pl.ds(16, 16)])
        theirs = pl.ds(pl.multiple_of((1 - core) * COLS, COLS), COLS)
        copy(N_SHARE, j, n_anti.at[j, :, :, theirs], n_other.at[j], to_sib).start()

    def pass_grad(j):
        arrived(HG_ANTI, j, hg_anti.at[j])
        copy(HG_FWD, j, hg_anti.at[j], hg_other.at[j], to_sib).start()

    def stage(run, j):
        pl.when(jnp.logical_and(j >= 0, j < CH))(lambda: run(j))

    def turn(i, _):
        stage(carry_on, i - 6)
        stage(give_rows, i - 7)
        stage(pass_grad, i - 19)
        stage(relay_normed, i - 9)
        stage(choose, i)
        stage(spread_normed, i - 6)
        stage(relay, i - 1)
        stage(backward, i - 7)
        stage(far_sum, i - 3)
        stage(send_grads, i - 7)
        stage(forward, i - 2)
        stage(add_row_halves, i - 10)
        stage(row_sums, i - 7)
        stage(send_normed, i - 2)
        stage(near_sums, i - 3)
        stage(add_halves, i - 4)
        stage(share_normed, i - 18)
        return 0

    lax.fori_loop(0, CH + 19, turn, 0)

    def last_arrivals(j, _):
        arrived(HG_SIB, j, hg_sib.at[j])
        arrived(HG_FWD, j, hg_other.at[j])
        arrived(N_SIB, j, n_sib.at[j])
        arrived(N_SHARE, j, n_other.at[j])
        return 0

    lax.fori_loop(0, CH, last_arrivals, 0)
    for load in moments:
        load.wait()

    def product(left_rows, right_rows):
        return lax.dot_general(
            left_rows.reshape(CH * ROWS, TILE), right_rows.reshape(CH * ROWS, 512),
            (((0,), (0,)), ((), ())), preferred_element_type=jnp.float32,
        )

    def step_dir(q, _):
        f = q // 2
        rows = pl.ds(pl.multiple_of(f * TILE, TILE), TILE)
        there = pl.ds(pl.multiple_of(lax.rem(q, 2) * 512, 512), 512)
        total = product(nrm[:, :, :, tile(d, f)], hg[:, :, there])
        total += product(n_sib[:, :, :, rows], hg_sib[:, :, there])
        total += product(n_anti[:, :, :, tile(core, f)], hg_anti[:, :, there])
        total += product(n_other[:, :, :, rows], hg_other[:, :, there])
        total = total * (1.0 / (4 * CH * ROWS))
        pair = pl.ds(lax.rem(f, 2) * 2, 2)
        one = f32(x_all[f // 2, pair, :, :, there]).reshape(TILE, 512)
        two = f32(x_all[2 + f // 2, pair, :, :, there]).reshape(TILE, 512)
        first = BETA_ONE * one + (1.0 - BETA_ONE) * total
        second = BETA_TWO * two + (1.0 - BETA_TWO) * total * total
        value = bf16(first / (jnp.sqrt(second) + 1e-08))
        x_all[f // 2, pair, :, :, there] = value.reshape(2, 4, SLAB, 512)
        return 0

    lax.fori_loop(0, 8, step_dir, 0)
    out = pltpu.make_async_copy(x_all.at[0:2], upd_ref, local_sem.at[14])
    out.start()
    lax.fori_loop(0, CH, lambda j, _: (finish_rows(j), 0)[1], 0)

    def drain(j, _):
        for k in range(1, 4):
            arrived(Y_ONE + k - 1, j, y_ref.at[j, :, cols(lax.rem(t + 4 - k, 4))])
            sent(Y_ONE + k - 1, j, y_cols.at[j, 0])
        pltpu.make_async_copy(y_cols.at[j, t], y_ref.at[j, :, cols(t)], local_sem.at[6 + j]).wait()
        pltpu.make_async_copy(row_l.at[j], dx_ref.at[j], local_sem.at[10 + j]).wait()
        for q in range(3):
            sent(X_ONE + q, j, x_all.at[j, :, t])
        sent(GATHER_R, j, in_all.at[j, pl.ds(0, 64), cols(t)])
        sent(HIGH_R, j, in_all.at[j, pl.ds(64, 64), cols(t)])
        sent(LOW_L, j, in_all.at[j, pl.ds(0, 64), cols(t)])
        sent(GATHER_L, j, in_all.at[j, pl.ds(64, 64), cols(t)])
        sent(RELAY_R, j, in_all.at[j, pl.ds(0, 64), cols(left)])
        sent(RELAY_L, j, in_all.at[j, pl.ds(64, 64), cols(right)])
        sent(OPP_R, j, opp.at[j, pl.ds(0, 64)])
        sent(OPP_L, j, opp.at[j, pl.ds(64, 64)])
        sent(SUM_R, j, to_r.at[j])
        sent(SUM_L, j, to_l.at[j])
        sent(CARRY_MOVE, j, own.at[j])
        sent(ROW_OPP_R, j, part.at[j, across, pl.ds(0, 16)])
        sent(ROW_OPP_L, j, part.at[j, across, pl.ds(16, 16)])
        sent(ROW_SUM_R, j, part.at[j, right])
        sent(ROW_SUM_L, j, part.at[j, left])
        sent(HG_SIB, j, hg.at[j])
        sent(HG_ANTI, j, hg.at[j])
        sent(HG_FWD, j, hg_anti.at[j])
        sent(N_ANTI, j, n_anti.at[j, t])
        sent(N_SIB, j, n_sib.at[j])
        sent(N_R, j, n_anti.at[j, t])
        sent(N_L, j, n_anti.at[j, t])
        sent(N_RELAY_R, j, n_anti.at[j, left, pl.ds(0, 16)])
        sent(N_RELAY_L, j, n_anti.at[j, right, pl.ds(16, 16)])
        sent(N_SHARE, j, n_other.at[j])
        return 0

    lax.fori_loop(0, CH, drain, 0)
    sent(W_SIB, 0, w_all.at[cols(d)])
    for k in range(3):
        sent(C_COLS, k, cot.at[:, t])
        sent(W_ANTI, k, w_all.at[cols(d), quarter(k)])
        sent(W_FWD, k, w_all.at[cols(anti), quarter(k)])
    for kind, onward, index, at, there in pieces:
        sent(kind, index, w_all.at[cols(d), there])
        sent(onward, at, w_all.at[cols(anti), there])
    out.wait()


def whole(x, cot, w, m1, m2, gain, flags):
    def vm(*shape, dtype=jnp.bfloat16):
        return pltpu.VMEM(shape, dtype)

    scratch = [
        vm(D, COLS), vm(COLS, D), vm(4, CH, 4, SLAB, COLS), vm(CH, ROWS, D), vm(CH, 4, SLAB, D),
        vm(CH, ROWS, COLS, dtype=jnp.float32), vm(CH, 4, SLAB, COLS),
        vm(CH, 4, SLAB, COLS), vm(CH, ROWS, COLS), vm(CH, 4, SLAB, COLS),
        vm(CH, ROWS, COLS), vm(CH, ROWS, COLS), vm(CH, ROWS, COLS), vm(CH, ROWS, COLS),
        vm(CH, 64, COLS), vm(CH, 64, COLS), vm(CH, ROWS, COLS), vm(CH, ROWS, COLS),
        vm(CH, 4, SLAB, D), vm(CH, 16, D), vm(CH, 16, D), vm(CH, SLAB, D), vm(CH, SLAB, D),
        vm(CH, ROWS, COLS), vm(CH, ROWS, COLS), vm(CH, ROWS, COLS), vm(CH, ROWS, COLS),
        vm(CH, 4, SLAB, COLS), vm(CH, 4, SLAB, 2 * COLS), vm(CH, 4, SLAB, COLS),
        vm(CH, ROWS, 1, dtype=jnp.float32), vm(CH, ROWS, 1, dtype=jnp.float32),
        pltpu.SemaphoreType.DMA((37, CH)), pltpu.SemaphoreType.DMA((37, CH)), pltpu.SemaphoreType.DMA((15,)),
    ]
    anywhere = pl.BlockSpec(memory_space=pl.ANY)
    near = pl.BlockSpec(memory_space=pltpu.VMEM)
    return pl.pallas_call(
        kernel,
        out_shape=(
            jax.ShapeDtypeStruct((CH, SLAB, D), jnp.bfloat16),
            jax.ShapeDtypeStruct((CH, SLAB, D), jnp.bfloat16),
            jax.ShapeDtypeStruct((2, 4, 4, SLAB, COLS), jnp.bfloat16),
        ),
        in_specs=[anywhere] * 5 + [near, pl.BlockSpec(memory_space=pltpu.SMEM)],
        out_specs=(anywhere,) * 3,
        scratch_shapes=scratch,
        compiler_params=pltpu.CompilerParams(
            collective_id=0, has_side_effects=True, vmem_limit_bytes=63 * 2**20
        ),
        cost_estimate=pl.CostEstimate(flops=21 * 10**9, bytes_accessed=20 * 2**20, transcendentals=2 * 10**6),
    )(x, cot, w, m1, m2, gain, flags)


def body(x_in, gain, weight, moment_one, moment_two, cotangent, preempted):
    y, dx, update = whole(
        x_in.reshape(CH, SLAB, D), cotangent.reshape(CH, SLAB, D), weight[0],
        moment_one.reshape(2, 4, 4, SLAB, COLS), moment_two.reshape(2, 4, 4, SLAB, COLS), gain, preempted,
    )
    return (y.reshape(1, CH * SLAB, D), dx.reshape(1, CH * SLAB, D), update.reshape(1, COLS, COLS))


def solution(mesh):
    placed = (
        P("section", ("dp", "tensor"), None),
        P("section", None),
        P("section", "dp", "tensor"),
        P("section", "dp", "tensor"),
        P("section", "dp", "tensor"),
        P("section", ("dp", "tensor"), None),
        P(),
    )
    return jax.shard_map(
        body,
        mesh=mesh,
        in_specs=placed,
        out_specs=(
            P("section", ("dp", "tensor"), None),
            P("section", ("dp", "tensor"), None),
            P("section", "dp", "tensor"),
        ),
        check_vma=False,
    )
```
